32 devices in a mesh: ctx: 8 (over z, x), dp: 4 (over y, core).
Axes of the slice: x: 2, y: 2, z: 4, core: 2. Of those that a mesh axis runs over, the one named last changes fastest.
Arguments:
- query: bfloat16 [4, 4096, 1024], P('dp', 'ctx'), may hold values from -6 to 6
- key: bfloat16 [4, 4096, 1024], P('dp', 'ctx'), may hold values from -6 to 6
- value: bfloat16 [4, 4096, 1024], P('dp', 'ctx'), may hold values from -12 to 12
- log_decay: float32 [4, 8, 4096], P('dp', None, 'ctx'), may hold values from -2 to 0
- grad_out: bfloat16 [4, 4096, 1024], P('dp', 'ctx'), may hold values from -32 to 32
- query_map: bfloat16 [8, 128, 128], replicated, may hold values from -0.5 to 0.5
- key_map: bfloat16 [8, 128, 128], replicated, may hold values from -0.5 to 0.5
Outputs:
- output: bfloat16 [4, 4096, 1024], P('dp', 'ctx')
- grad_query: bfloat16 [4, 4096, 1024], P('dp', 'ctx')
- grad_key: bfloat16 [4, 4096, 1024], P('dp', 'ctx')
- grad_value: bfloat16 [4, 4096, 1024], P('dp', 'ctx')
- query_map_grad: float32 [8, 128, 128], replicated
- key_map_grad: float32 [8, 128, 128], replicated
The draws below stay inside these ranges and needn't reach their ends.
All inputs are finite; a program needn't handle non-finite values.
Results may differ from the reference program's by a relative error of at most 0.0073.
Values sent between devices are 32-bit elements; how exact they have to be, the bound alone decides.
A program may use at most 128 MiB of HBM per device.

```python
import math
import jax
import jax.numpy as jnp
from jax import lax

LOCAL_HEADS = 8
DH = 128
BLOCK = 256
TOK_DEV = 512
SEQUENCE_LENGTH = 4096
BATCH_SEQUENCES = 4


def decay_plan(key):
    plan_keys = jax.random.split(jax.random.fold_in(key, 7001), 4)
    array_shape = (BATCH_SEQUENCES, LOCAL_HEADS, 1)
    kind_draw = jax.random.randint(plan_keys[0], array_shape, 0, 20)
    fast_limit = 5
    medium_limit = 10
    is_fast = kind_draw < fast_limit
    is_medium = jnp.logical_and(kind_draw >= fast_limit, kind_draw < medium_limit)
    fast_rate = jnp.exp(jax.random.uniform(plan_keys[1], array_shape, jnp.float32, math.log(7.75), math.log(8.53))) / BLOCK
    medium_rate = -jax.random.uniform(plan_keys[2], array_shape, jnp.float32, math.log(0.035), math.log(0.045)) / TOK_DEV
    slow_rate = jnp.exp(jax.random.uniform(plan_keys[3], array_shape, jnp.float32, math.log(0.4), math.log(1.0))) / SEQUENCE_LENGTH
    decay_rate = jnp.where(is_fast, fast_rate, jnp.where(is_medium, medium_rate, slow_rate))
    rate_spread = jnp.where(is_medium, 0.12, 0.35)
    memory_span = jnp.minimum(0.5 / decay_rate, 0.5 * SEQUENCE_LENGTH)
    head_scale = jnp.minimum(3.0, 12.0 / jnp.sqrt(memory_span))
    return (decay_rate, rate_spread, head_scale, is_medium)


def shard_factors(key):
    phase_draw = jax.random.randint(jax.random.fold_in(key, 7002), (BATCH_SEQUENCES, 1), 0, 3)
    shard_kind = (jnp.arange(SEQUENCE_LENGTH)[None, :] // TOK_DEV + phase_draw) % 3
    value_factor = jnp.where(shard_kind == 0, 1.0, 0.125)
    grad_factor = jnp.where(shard_kind == 0, 1.0, jnp.where(shard_kind == 1, 0.125, 8.0))
    return (value_factor, grad_factor)


def column_spread(per_head):
    spread_out = jnp.broadcast_to(per_head, (BATCH_SEQUENCES, LOCAL_HEADS, DH))
    return spread_out.reshape(BATCH_SEQUENCES, 1, LOCAL_HEADS * DH)


def unit_noise(noise_key, array_shape):
    return jnp.clip(jax.random.normal(noise_key, array_shape, jnp.float32), -4.0, 4.0)


def draw_value(key, part):
    _, _, head_scale, is_medium = decay_plan(key)
    value_factor, _ = shard_factors(key)
    noise = unit_noise(jax.random.fold_in(key, 7004), (BATCH_SEQUENCES, SEQUENCE_LENGTH, LOCAL_HEADS * DH))
    medium_cols = column_spread(is_medium.astype(jnp.float32))
    shard_scale = 1.0 + medium_cols * (value_factor[:, :, None] - 1.0)
    return (noise * column_spread(head_scale) * shard_scale).astype(jnp.bfloat16)


def draw_grad_out(key, part):
    _, _, _, is_medium = decay_plan(key)
    _, grad_factor = shard_factors(key)
    noise = unit_noise(jax.random.fold_in(key, 7005), (BATCH_SEQUENCES, SEQUENCE_LENGTH, LOCAL_HEADS * DH))
    medium_cols = column_spread(is_medium.astype(jnp.float32))
    shard_scale = 1.0 + medium_cols * (grad_factor[:, :, None] - 1.0)
    return (noise * shard_scale).astype(jnp.bfloat16)


def draw_log_decay(key, part):
    decay_rate, rate_spread, _, _ = decay_plan(key)
    key_list = jax.random.split(jax.random.fold_in(key, 7003), 4)
    shard_count = SEQUENCE_LENGTH // TOK_DEV
    device_factor = jnp.exp(rate_spread[..., None] * jax.random.uniform(key_list[0], (BATCH_SEQUENCES, LOCAL_HEADS, shard_count, 1), jnp.float32, -1.0, 1.0))
    device_factor = jnp.broadcast_to(device_factor, (BATCH_SEQUENCES, LOCAL_HEADS, shard_count, TOK_DEV)).reshape(BATCH_SEQUENCES, LOCAL_HEADS, SEQUENCE_LENGTH)
    token_factor = jax.random.uniform(key_list[1], (BATCH_SEQUENCES, LOCAL_HEADS, SEQUENCE_LENGTH), jnp.float32, 0.5, 1.5)
    token_positions = jax.random.randint(key_list[2], (BATCH_SEQUENCES, 1, 3), 0, SEQUENCE_LENGTH)
    loss_values = jax.random.uniform(key_list[3], (BATCH_SEQUENCES, LOCAL_HEADS, 3), jnp.float32, 0.2, 0.5)
    shard_places = jnp.arange(SEQUENCE_LENGTH)[None, None, :]
    spike_record = jnp.zeros((BATCH_SEQUENCES, LOCAL_HEADS, SEQUENCE_LENGTH), jnp.float32)
    for spike_index in range(3):
        spike_record = spike_record + jnp.where(shard_places == token_positions[:, :, spike_index:spike_index + 1], jnp.log(1.0 - loss_values[:, :, spike_index:spike_index + 1]), 0.0)
    return jnp.maximum(-(decay_rate * device_factor * token_factor) + spike_record, -2.0)


def levels(key, extent, cuts, least, top_value):
    factor_of = 1.0
    for dim, blocks in cuts:
        steps = jax.random.uniform(jax.random.fold_in(jax.random.fold_in(key, 6), dim), (blocks,), jnp.float32, least / len(cuts), top_value / len(cuts))
        factor_of = factor_of * jnp.repeat(jnp.exp(steps), extent[dim] // blocks).reshape((-1,) + (1,) * (len(extent) - 1 - dim))
    return factor_of


def normal_values(own_key, shape, scale, bound, cuts=(), kind=jnp.bfloat16):
    result = jax.random.normal(own_key, shape, jnp.float32) * scale
    if len(cuts) > 0:
        result = levels(own_key, shape, cuts, -0.22, 0.18) * result
    return jnp.clip(result, min=-bound, max=bound).astype(kind)


def setup_inputs(seed: int = 0) -> dict:
    key_of = jax.random.split(jax.random.key(seed), 8)
    query = normal_values(key_of[0], (BATCH_SEQUENCES, SEQUENCE_LENGTH, LOCAL_HEADS * DH), 1.0, 6.0, ((0, 4), (1, 8)))
    key = normal_values(key_of[1], (BATCH_SEQUENCES, SEQUENCE_LENGTH, LOCAL_HEADS * DH), 1.0, 6.0, ((0, 4), (1, 8)))
    value = draw_value(jax.random.fold_in(key_of[7], 71), 0)
    log_decay = draw_log_decay(jax.random.fold_in(key_of[7], 71), 0)
    grad_out = draw_grad_out(jax.random.fold_in(key_of[7], 71), 0)
    query_map = normal_values(key_of[5], (LOCAL_HEADS, DH, DH), DH ** -0.5, 0.5)
    key_map = normal_values(key_of[6], (LOCAL_HEADS, DH, DH), DH ** -0.5, 0.5)
    return dict(query=query, key=key, value=value, log_decay=log_decay, grad_out=grad_out, query_map=query_map, key_map=key_map)


def silu_slope(pre_act):
    sigmoid_val = jax.nn.sigmoid(pre_act)
    return sigmoid_val * (1.0 + pre_act * (1.0 - sigmoid_val))

def feature_map(inputs, weight, block_len):
    head_count, head_width = (weight.shape[0], weight.shape[1])
    split_in = inputs.reshape(inputs.shape[0], head_count, head_width)
    pre_act = jnp.einsum('lhd,hde->hle', split_in.astype(jnp.float32), weight.astype(jnp.float32))
    features_out = jax.nn.silu(pre_act).astype(jnp.bfloat16)
    return (pre_act, features_out.reshape(head_count, -1, block_len, head_width))

def heads_blocks(array, head_count, block_len):
    rows = array.shape[0]
    return array.reshape(rows // block_len, block_len, head_count, -1).transpose(2, 0, 1, 3)

def unblock(array):
    head_count, block_count, block_len, head_width = array.shape
    return array.transpose(1, 2, 0, 3).reshape(block_count * block_len, head_count * head_width)

def chain_states(totals, updates):

    def advance(state, pieces):
        total_now, update_now = pieces
        return (jnp.exp(total_now)[:, None, None] * state + update_now, state)
    start = jnp.zeros((updates.shape[0], updates.shape[2], updates.shape[3]), jnp.float32)
    _, stacked = lax.scan(advance, start, (totals.T, updates.transpose(1, 0, 2, 3)))
    return stacked.transpose(1, 0, 2, 3)

def chain_adjoints(totals, contribs):

    def retreat(adjoint, pieces):
        total_now, contrib_now = pieces
        return (contrib_now + jnp.exp(total_now)[:, None, None] * adjoint, adjoint)
    start = jnp.zeros((contribs.shape[0], contribs.shape[2], contribs.shape[3]), jnp.float32)
    _, stacked = lax.scan(retreat, start, (totals.T, contribs.transpose(1, 0, 2, 3)), reverse=True)
    return stacked.transpose(1, 0, 2, 3)

def one_sequence(query_map, key_map, pieces):
    query, key, value, log_decay, grad_out = pieces
    head_count, head_width = (query_map.shape[0], query_map.shape[1])
    tokens = query.shape[0]
    out_scale = 1.0 / (head_width * math.sqrt(BLOCK))
    pre_query, query_feat = feature_map(query, query_map, BLOCK)
    pre_key, key_feat = feature_map(key, key_map, BLOCK)
    value_heads = heads_blocks(value, head_count, BLOCK)
    grad_heads = heads_blocks(grad_out, head_count, BLOCK)
    cumulative = jnp.cumsum(log_decay.reshape(head_count, -1, BLOCK), axis=-1)
    totals = cumulative[..., -1]
    causal_mask = jnp.arange(BLOCK)[:, None] >= jnp.arange(BLOCK)[None, :]
    differ = cumulative[..., :, None] - cumulative[..., None, :]
    weights = jnp.where(causal_mask, jnp.exp(jnp.where(causal_mask, differ, 0.0)), 0.0)
    query_wide = query_feat.astype(jnp.float32)
    key_wide = key_feat.astype(jnp.float32)
    value_wide = value_heads.astype(jnp.float32)
    grad_wide = grad_heads.astype(jnp.float32)
    scores = jnp.einsum('hnsd,hntd->hnst', query_wide, key_wide)
    block_probs = (scores * weights).astype(jnp.bfloat16)
    intra_out = jnp.einsum('hnst,hntd->hnsd', block_probs.astype(jnp.float32), value_wide)
    key_dec = (key_wide * jnp.exp(totals[..., None] - cumulative)[..., None]).astype(jnp.bfloat16)
    query_dec = (query_wide * jnp.exp(cumulative)[..., None]).astype(jnp.bfloat16)
    updates = jnp.einsum('hntd,hnte->hnde', key_dec.astype(jnp.float32), value_wide)
    state_round = chain_states(totals, updates).astype(jnp.bfloat16).astype(jnp.float32)
    inter_out = jnp.einsum('hnsd,hnde->hnse', query_dec.astype(jnp.float32), state_round)
    output = (out_scale * (intra_out + inter_out)).astype(jnp.bfloat16)
    contribs = jnp.einsum('hnsd,hnse->hnde', query_dec.astype(jnp.float32), grad_wide)
    after_round = chain_adjoints(totals, contribs).astype(jnp.bfloat16).astype(jnp.float32)
    grad_scores = (jnp.einsum('hnse,hnte->hnst', grad_wide, value_wide) * weights).astype(jnp.bfloat16)
    score_wide = grad_scores.astype(jnp.float32)
    grad_value = out_scale * (jnp.einsum('hnst,hnsd->hntd', block_probs.astype(jnp.float32), grad_wide) + jnp.einsum('hntd,hnde->hnte', key_dec.astype(jnp.float32), after_round))
    grad_qfeat = out_scale * (jnp.einsum('hnst,hntd->hnsd', score_wide, key_wide) + jnp.exp(cumulative)[..., None] * jnp.einsum('hnse,hnde->hnsd', grad_wide, state_round))
    grad_kfeat = out_scale * (jnp.einsum('hnst,hnsd->hntd', score_wide, query_wide) + jnp.exp(totals[..., None] - cumulative)[..., None] * jnp.einsum('hnte,hnde->hntd', value_wide, after_round))
    grad_pre_query = (grad_qfeat.reshape(head_count, tokens, head_width) * silu_slope(pre_query)).astype(jnp.bfloat16)
    grad_pre_key = (grad_kfeat.reshape(head_count, tokens, head_width) * silu_slope(pre_key)).astype(jnp.bfloat16)
    grad_query = jnp.einsum('hle,hde->lhd', grad_pre_query.astype(jnp.float32), query_map.astype(jnp.float32)).astype(jnp.bfloat16)
    grad_key = jnp.einsum('hle,hde->lhd', grad_pre_key.astype(jnp.float32), key_map.astype(jnp.float32)).astype(jnp.bfloat16)
    query_part = jnp.einsum('lhd,hle->hde', query.reshape(tokens, head_count, head_width).astype(jnp.float32), grad_pre_query.astype(jnp.float32))
    key_part = jnp.einsum('lhd,hle->hde', key.reshape(tokens, head_count, head_width).astype(jnp.float32), grad_pre_key.astype(jnp.float32))
    return (unblock(output), grad_query.reshape(tokens, -1), grad_key.reshape(tokens, -1), unblock(grad_value.astype(jnp.bfloat16)), query_part, key_part)

def reference(query, key, value, log_decay, grad_out, query_map, key_map):

    def per_sequence(pieces):
        return one_sequence(query_map, key_map, pieces)
    results = lax.map(per_sequence, (query, key, value, log_decay, grad_out))
    return (results[0], results[1], results[2], results[3], lax.optimization_barrier(jnp.sum(results[4], axis=0)), lax.optimization_barrier(jnp.sum(results[5], axis=0)))
```

```python
import functools
import math

import jax
import jax.numpy as jnp
from jax import lax
from jax.experimental import pallas as pl
from jax.experimental.pallas import tpu as pltpu
from jax.sharding import PartitionSpec as P

BLOCK = 256
MESH = pl.DeviceIdType.MESH
F32 = jnp.float32
BF16 = jnp.bfloat16


def mm(a, b):
    return lax.dot_general(a, b, (((1,), (0,)), ((), ())), preferred_element_type=F32)


def mm_nt(a, b):
    return lax.dot_general(a, b, (((1,), (1,)), ((), ())), preferred_element_type=F32)


def mm_tn(a, b):
    return lax.dot_general(a, b, (((0,), (0,)), ((), ())), preferred_element_type=F32)


def sigmoid(u):
    return 1.0 / (1.0 + jnp.exp(-u))


def kernel(
    n, nd, heads, width, tokens,
    q_h, k_h, v_h, ld_ref, g_h, qm_ref, km_ref,
    o_h, gq_h, gk_h, gv_h, res_h,
    q_s, k_s, v_s, g_s, o_s, gq_s, gk_s, gv_s,
    preq_s, prek_s, qf_s, kf_s, qd_s, kd_s,
    cum_s, col_s, mine_s, theirs_s,
    U_s, C_s, u0_s, c1_s, fin_s, fout_s, xout_s, xin_s,
    part_s, pin_s, own_s, cin_s, res_s,
    in_sem, out_sem, dec_sem, ch_send, ch_recv, x_send, x_recv,
    p_send, p_recv, c_send, c_recv, ag_send, ag_recv,
    y_send, y_recv, k_send, k_recv,
):
    scale = 1.0 / (width * math.sqrt(BLOCK))
    me = lax.axis_index("ctx")
    d = lax.axis_index("dp")
    nz = n // 2
    z = me // 2
    x = lax.rem(me, 2)
    partner = me + 1 - 2 * x
    rows = width // nd

    loads = [
        pltpu.make_async_copy(src, dst, in_sem.at[i])
        for i, (src, dst) in enumerate(((k_h, k_s), (v_h, v_s), (q_h, q_s), (g_h, g_s)))
    ]
    for copy in loads:
        copy.start()

    barrier = pltpu.get_barrier_semaphore()

    @pl.loop(1, n)
    def _(r):
        pl.semaphore_signal(
            barrier, inc=1, device_id=(lax.rem(me + r, n), d), device_id_type=MESH
        )

    for r in range(1, nd):
        pl.semaphore_signal(
            barrier, inc=1, device_id=(me, lax.rem(d + r, nd)), device_id_type=MESH
        )

    cum = ld_ref[...]
    lane = lax.rem(lax.broadcasted_iota(jnp.int32, cum.shape, 1), BLOCK)
    shift = 1
    while shift < BLOCK:
        cum = cum + jnp.where(lane >= shift, pltpu.roll(cum, shift, 1), 0.0)
        shift *= 2
    cum_s[...] = cum
    last = cum[:, BLOCK - 1 : BLOCK] + cum[:, 2 * BLOCK - 1 : 2 * BLOCK]
    mine_s[...] = jnp.broadcast_to(last, mine_s.shape)

    @pl.when(z == 0)
    def _():
        fin_s[0] = jnp.zeros_like(fin_s[0])

    @pl.when(z == nz - 1)
    def _():
        fin_s[1] = jnp.zeros_like(fin_s[1])

    pl.semaphore_wait(barrier, n - 1 + nd - 1)
    decay_copy = pltpu.make_async_remote_copy(
        src_ref=mine_s, dst_ref=theirs_s, send_sem=dec_sem.at[0], recv_sem=dec_sem.at[1],
        device_id=(partner, d), device_id_type=MESH,
    )
    decay_copy.start()
    for copy in loads:
        copy.wait()
    decay_copy.wait()

    def cols(h):
        return pl.ds(pl.multiple_of(h * width, width), width)

    def blk(b):
        return pl.ds(b * BLOCK, BLOCK)

    def first_pass(h):
        c = cols(h)
        pre = mm(k_s[:, c], km_ref[h])
        prek_s[:, c] = pre
        kf_s[:, c] = (pre * sigmoid(pre)).astype(BF16)
        pre = mm(q_s[:, c], qm_ref[h])
        preq_s[:, c] = pre
        qf_s[:, c] = (pre * sigmoid(pre)).astype(BF16)
        col = jnp.broadcast_to(cum_s[pl.ds(h, 1), :], (width, tokens)).T
        col_s[h] = col
        u, w = [], []
        for b in range(2):
            cb = col[b * BLOCK : (b + 1) * BLOCK]
            tot = cb[BLOCK - 1 : BLOCK]
            kd = (kf_s[blk(b), c].astype(F32) * jnp.exp(tot - cb)).astype(BF16)
            kd_s[blk(b), c] = kd
            u.append(mm_tn(kd, v_s[blk(b), c]))
            qd = (qf_s[blk(b), c].astype(F32) * jnp.exp(cb)).astype(BF16)
            qd_s[blk(b), c] = qd
            w.append(mm_tn(qd, g_s[blk(b), c]))
        d0 = jnp.exp(col[BLOCK - 1 : BLOCK])
        d1 = jnp.exp(col[2 * BLOCK - 1 : 2 * BLOCK])
        U_s[h] = d1 * u[0] + u[1]
        u0_s[h] = u[0]
        C_s[h] = w[0] + d0 * w[1]
        c1_s[h] = w[1]

    def chain_copy(way, h):
        to = z + 1 if way == 0 else z - 1
        to = jnp.clip(to, 0, nz - 1) * 2 + x
        return pltpu.make_async_remote_copy(
            src_ref=fout_s.at[way, h], dst_ref=fin_s.at[way, h],
            send_sem=ch_send.at[way, h], recv_sem=ch_recv.at[way, h],
            device_id=(to, d), device_id_type=MESH,
        )

    def cross_copy(way, h):
        return pltpu.make_async_remote_copy(
            src_ref=xout_s.at[way, h], dst_ref=xin_s.at[way, h],
            send_sem=x_send.at[way, h], recv_sem=x_recv.at[way, h],
            device_id=(partner, d), device_id_type=MESH,
        )

    def is_first(way):
        return (x == 0) if way == 0 else (x == 1)

    def has_in(way):
        return (z > 0) if way == 0 else (z < nz - 1)

    def has_out(way):
        return (z < nz - 1) if way == 0 else (z > 0)

    def chain(way, h):
        @pl.when(has_in(way))
        def _():
            chain_copy(way, h).wait_recv()

        own = mine_s[pl.ds(h, 1), :]
        other = theirs_s[pl.ds(h, 1), :]
        state = fin_s[way, h]
        term = (U_s if way == 0 else C_s)[h]
        first = is_first(way)

        @pl.when(has_out(way))
        def _():
            carry = jnp.where(first, jnp.exp(other), 1.0)
            fout_s[way, h] = jnp.exp(own + other) * state + carry * term
            chain_copy(way, h).start()

        keep = jnp.where(first, jnp.exp(own), 1.0)
        xout_s[way, h] = keep * state + jnp.where(first, term, 0.0)
        cross_copy(way, h).start()

    def entering(way, h):
        cross_copy(way, h).wait_recv()
        other = theirs_s[pl.ds(h, 1), :]
        keep = jnp.where(is_first(way), 1.0, jnp.exp(other))
        return keep * fin_s[way, h] + xin_s[way, h]

    def part_copy(m, r):
        to = lax.rem(d + r, nd)
        return pltpu.make_async_remote_copy(
            src_ref=part_s.at[to, m], dst_ref=pin_s.at[r - 1, m],
            send_sem=p_send.at[r - 1, m], recv_sem=p_recv.at[r - 1, m],
            device_id=(me, to), device_id_type=MESH,
        )

    def send_part(m, part):
        for i in range(nd):
            part_s[i, m] = part[i * rows : (i + 1) * rows]
        for r in range(1, nd):
            part_copy(m, r).start()

    iota0 = lax.broadcasted_iota(jnp.int32, (BLOCK, BLOCK), 0)
    iota1 = lax.broadcasted_iota(jnp.int32, (BLOCK, BLOCK), 1)

    def wide(cb):
        return jnp.concatenate([cb] * (BLOCK // width), axis=1)

    def slope(pre):
        s = sigmoid(pre)
        return s * (1.0 + pre * (1.0 - s))

    def finish_q(h):
        c = cols(h)
        state = entering(0, h)
        d0 = jnp.exp(col_s[h, pl.ds(BLOCK - 1, 1), :])
        states = (state.astype(BF16), (d0 * state + u0_s[h]).astype(BF16))
        total = None
        for b in range(2):
            st = states[b]
            cb = col_s[h, blk(b), :]
            row = cum_s[pl.ds(h, 1), blk(b)]
            weight = jnp.exp(jnp.where(iota0 >= iota1, wide(cb) - row, -1e30))
            kf, v, g = kf_s[blk(b), c], v_s[blk(b), c], g_s[blk(b), c]
            probs = (mm_nt(qf_s[blk(b), c], kf) * weight).astype(BF16)
            o_s[blk(b), c] = (scale * (mm(probs, v) + mm(qd_s[blk(b), c], st))).astype(BF16)
            gs = (mm_nt(g, v) * weight).astype(BF16)
            gf = scale * (mm(gs, kf) + jnp.exp(cb) * mm_nt(g, st))
            gp = (gf * slope(preq_s[blk(b), c])).astype(BF16)
            gq_s[blk(b), c] = mm_nt(gp, qm_ref[h]).astype(BF16)
            p = mm_tn(q_s[blk(b), c], gp)
            total = p if total is None else total + p
        send_part(h, total)

    def finish_k(h):
        c = cols(h)
        after = entering(1, h)
        d1 = jnp.exp(col_s[h, pl.ds(2 * BLOCK - 1, 1), :])
        afters = ((c1_s[h] + d1 * after).astype(BF16), after.astype(BF16))
        total = None
        for b in range(2):
            af = afters[b]
            cb = col_s[h, blk(b), :]
            tot = cb[BLOCK - 1 : BLOCK]
            row = cum_s[pl.ds(h, 1), blk(b)]
            weight = jnp.exp(jnp.where(iota1 >= iota0, row - wide(cb), -1e30))
            qf, v, g = qf_s[blk(b), c], v_s[blk(b), c], g_s[blk(b), c]
            probs = (mm_nt(kf_s[blk(b), c], qf) * weight).astype(BF16)
            gv_s[blk(b), c] = (scale * (mm(probs, g) + mm(kd_s[blk(b), c], af))).astype(BF16)
            gs = (mm_nt(v, g) * weight).astype(BF16)
            gf = scale * (mm(gs, qf) + jnp.exp(tot - cb) * mm_nt(v, af))
            gp = (gf * slope(prek_s[blk(b), c])).astype(BF16)
            gk_s[blk(b), c] = mm_nt(gp, km_ref[h]).astype(BF16)
            p = mm_tn(k_s[blk(b), c], gp)
            total = p if total is None else total + p
        send_part(heads + h, total)

    def inside(h):
        return jnp.logical_and(h >= 0, h < heads)

    @pl.loop(0, heads + 2 * (nz - 1) + 2)
    def _(s):
        hf = s - 2 * z
        ha = s - 2 * (nz - 1 - z)

        @pl.when(s < heads)
        def _():
            first_pass(s)

        @pl.when(inside(hf))
        def _():
            chain(0, hf)

        @pl.when(inside(ha))
        def _():
            chain(1, ha)

        @pl.when(inside(hf - 2))
        def _():
            finish_q(hf - 2)

        @pl.when(inside(ha - 2))
        def _():
            finish_k(ha - 2)

    stores = [
        pltpu.make_async_copy(src, dst, out_sem.at[i])
        for i, (src, dst) in enumerate(((o_s, o_h), (gq_s, gq_h), (gk_s, gk_h), (gv_s, gv_h)))
    ]
    for copy in stores:
        copy.start()

    @pl.loop(0, 2 * heads)
    def _(m):
        total = part_s[d, m]
        for r in range(1, nd):
            part_copy(m, r).wait_recv()
            total = total + pin_s[r - 1, m]
        own_s[pl.ds(pl.multiple_of(m * rows, rows), rows), :] = total

    size = own_s.shape[0] // n

    def piece(i):
        return pl.ds(pl.multiple_of(i * size, size), size)

    def ctx_copy(r):
        to = lax.rem(me + r, n)
        return pltpu.make_async_remote_copy(
            src_ref=own_s.at[piece(to)], dst_ref=cin_s.at[r - 1],
            send_sem=c_send.at[r - 1], recv_sem=c_recv.at[r - 1],
            device_id=(to, d), device_id_type=MESH,
        )

    @pl.loop(1, n)
    def _(r):
        ctx_copy(r).start()

    res_s[d, piece(me)] = own_s[piece(me)]

    @pl.loop(1, n)
    def _(r):
        ctx_copy(r).wait_recv()
        res_s[d, piece(me)] = res_s[d, piece(me)] + cin_s[r - 1]

    def gather_copy(r):
        return pltpu.make_async_remote_copy(
            src_ref=res_s.at[d, piece(me)], dst_ref=res_s.at[d, piece(me)],
            send_sem=ag_send.at[r - 1], recv_sem=ag_recv.at[r - 1],
            device_id=(lax.rem(me + r, n), d), device_id_type=MESH,
        )

    def gather_arrival(r):
        at = piece(lax.rem(me + n - r, n))
        return pltpu.make_async_remote_copy(
            src_ref=res_s.at[d, at], dst_ref=res_s.at[d, at],
            send_sem=ag_send.at[r - 1], recv_sem=ag_recv.at[r - 1],
            device_id=(lax.rem(me + r, n), d), device_id_type=MESH,
        )

    across = lax.rem(d + 2, nd)
    beside = d + 1 - 2 * lax.rem(d, 2)
    diagonal = lax.rem(beside + 2, nd)

    def y_copy(r, whose):
        at = piece(lax.rem(me + n - r, n))
        return pltpu.make_async_remote_copy(
            src_ref=res_s.at[whose, at], dst_ref=res_s.at[whose, at],
            send_sem=y_send.at[r], recv_sem=y_recv.at[r],
            device_id=(me, across), device_id_type=MESH,
        )

    def core_copy(r, i, whose):
        at = piece(lax.rem(me + n - r, n))
        return pltpu.make_async_remote_copy(
            src_ref=res_s.at[whose, at], dst_ref=res_s.at[whose, at],
            send_sem=k_send.at[i, r], recv_sem=k_recv.at[i, r],
            device_id=(me, beside), device_id_type=MESH,
        )

    @pl.loop(1, n)
    def _(r):
        gather_copy(r).start()

    @pl.loop(0, n)
    def _(r):
        @pl.when(r > 0)
        def _():
            gather_arrival(r).wait_recv()

        y_copy(r, d).start()
        core_copy(r, 0, d).start()

    @pl.loop(0, n)
    def _(r):
        y_copy(r, across).wait_recv()
        core_copy(r, 1, across).start()

    @pl.loop(0, n)
    def _(r):
        core_copy(r, 0, beside).wait_recv()
        core_copy(r, 1, diagonal).wait_recv()

    result = pltpu.make_async_copy(res_s, res_h, out_sem.at[4])
    result.start()

    @pl.loop(0, heads)
    def _(h):
        for way in range(2):
            cross_copy(way, h).wait_send()

            @pl.when(has_out(way))
            def _():
                chain_copy(way, h).wait_send()

    @pl.loop(0, 2 * heads)
    def _(m):
        for r in range(1, nd):
            part_copy(m, r).wait_send()

    @pl.loop(1, n)
    def _(r):
        ctx_copy(r).wait_send()
        gather_copy(r).wait_send()

    @pl.loop(0, n)
    def _(r):
        y_copy(r, d).wait_send()
        core_copy(r, 0, d).wait_send()
        core_copy(r, 1, across).wait_send()

    for copy in stores:
        copy.wait()
    result.wait()


def solution(mesh):
    n, nd = mesh.shape["ctx"], mesh.shape["dp"]

    def local(query, key, value, log_decay, grad_out, query_map, key_map):
        heads, width = query_map.shape[0], query_map.shape[1]
        tokens = query.shape[1]
        wide = heads * width
        rows = width // nd
        owned = 2 * heads * rows
        any_spec = pl.BlockSpec(memory_space=pl.ANY)
        vmem_spec = pl.BlockSpec(memory_space=pltpu.VMEM)
        act = pltpu.VMEM((tokens, wide), BF16)
        act32 = pltpu.VMEM((tokens, wide), F32)
        mats = pltpu.VMEM((heads, width, width), F32)
        mats2 = pltpu.VMEM((2, heads, width, width), F32)
        dma = pltpu.SemaphoreType.DMA
        outs = pl.pallas_call(
            functools.partial(kernel, n, nd, heads, width, tokens),
            out_shape=[jax.ShapeDtypeStruct((tokens, wide), BF16)] * 4
            + [jax.ShapeDtypeStruct((nd, owned, width), F32)],
            in_specs=[any_spec, any_spec, any_spec, vmem_spec, any_spec, vmem_spec, vmem_spec],
            out_specs=[any_spec] * 5,
            scratch_shapes=[act] * 8
            + [act32] * 2
            + [act] * 4
            + [
                pltpu.VMEM((heads, tokens), F32),
                pltpu.VMEM((heads, tokens, width), F32),
                pltpu.VMEM((heads, width), F32),
                pltpu.VMEM((heads, width), F32),
            ]
            + [mats] * 4
            + [mats2] * 4
            + [
                pltpu.VMEM((nd, 2 * heads, rows, width), F32),
                pltpu.VMEM((nd - 1, 2 * heads, rows, width), F32),
                pltpu.VMEM((owned, width), F32),
                pltpu.VMEM((n - 1, owned // n, width), F32),
                pltpu.VMEM((nd, owned, width), F32),
            ]
            + [
                dma((4,)),
                dma((5,)),
                dma((2,)),
                dma((2, heads)),
                dma((2, heads)),
                dma((2, heads)),
                dma((2, heads)),
                dma((nd - 1, 2 * heads)),
                dma((nd - 1, 2 * heads)),
                dma((n - 1,)),
                dma((n - 1,)),
                dma((n - 1,)),
                dma((n - 1,)),
                dma((n,)),
                dma((n,)),
                dma((2, n)),
                dma((2, n)),
            ],
            compiler_params=pltpu.CompilerParams(
                collective_id=0, has_side_effects=True, vmem_limit_bytes=48 * 1024 * 1024
            ),
            cost_estimate=pl.CostEstimate(
                flops=4_000_000_000, bytes_accessed=10_000_000, transcendentals=4_000_000
            ),
        )(query[0], key[0], value[0], log_decay[0], grad_out[0], query_map, key_map)
        maps = outs[4].reshape(nd, 2, heads, rows, width).transpose(1, 2, 0, 3, 4)
        maps = maps.reshape(2, heads, width, width)
        return (outs[0][None], outs[1][None], outs[2][None], outs[3][None], maps[0], maps[1])

    return jax.shard_map(
        local,
        mesh=mesh,
        in_specs=(
            P("dp", "ctx", None),
            P("dp", "ctx", None),
            P("dp", "ctx", None),
            P("dp", None, "ctx"),
            P("dp", "ctx", None),
            P(),
            P(),
        ),
        out_specs=(
            P("dp", "ctx", None),
            P("dp", "ctx", None),
            P("dp", "ctx", None),
            P("dp", "ctx", None),
            P(),
            P(),
        ),
        check_vma=False,
    )
```

```python
import functools
import math

import jax
import jax.numpy as jnp
from jax import lax
from jax.experimental import pallas as pl
from jax.experimental.pallas import tpu as pltpu
from jax.sharding import PartitionSpec as P

BLOCK = 256
MESH = pl.DeviceIdType.MESH
F32 = jnp.float32
BF16 = jnp.bfloat16


def mm(a, b):
    return lax.dot_general(a, b, (((1,), (0,)), ((), ())), preferred_element_type=F32)


def mm_nt(a, b):
    return lax.dot_general(a, b, (((1,), (1,)), ((), ())), preferred_element_type=F32)


def mm_tn(a, b):
    return lax.dot_general(a, b, (((0,), (0,)), ((), ())), preferred_element_type=F32)


def sigmoid(u):
    return 1.0 / (1.0 + jnp.exp(-u))


def kernel(
    n, nd, groups, heads, width, tokens,
    q_h, k_h, v_h, ld_ref, g_h, qm_ref, km_ref,
    o_h, gq_h, gk_h, gv_h, res_h,
    q_s, k_s, v_s, g_s, o_s, gq_s, gk_s, gv_s,
    sq_s, sk_s, qf_s, kf_s, qd_s, kd_s,
    cum_s, col_s, eq_s, ek_s, mine_s, theirs_s,
    U_s, C_s, u0_s, c1_s, fin_s, fout_s, xout_s, xin_s,
    part_s, pin_s, own_s, cin_s, res_s,
    in_sem, out_sem, dec_sem, ch_send, ch_recv, x_send, x_recv,
    p_send, p_recv, c_send, c_recv, ag_send, ag_recv,
    y_send, y_recv, k_send, k_recv,
):
    scale = 1.0 / (width * math.sqrt(BLOCK))
    me = lax.axis_index("ctx")
    d = lax.axis_index("dp")
    nz = n // 2
    z = me // 2
    x = lax.rem(me, 2)
    partner = me + 1 - 2 * x
    rows = width // nd
    hh = heads // groups

    loads = [
        pltpu.make_async_copy(src, dst, in_sem.at[i])
        for i, (src, dst) in enumerate(((k_h, k_s), (v_h, v_s), (q_h, q_s), (g_h, g_s)))
    ]
    for copy in loads:
        copy.start()

    barrier = pltpu.get_barrier_semaphore()

    @pl.loop(1, n)
    def _(r):
        pl.semaphore_signal(
            barrier, inc=1, device_id=(lax.rem(me + r, n), d), device_id_type=MESH
        )

    for r in range(1, nd):
        pl.semaphore_signal(
            barrier, inc=1, device_id=(me, lax.rem(d + r, nd)), device_id_type=MESH
        )

    cum = ld_ref[...]
    lane = lax.rem(lax.broadcasted_iota(jnp.int32, cum.shape, 1), BLOCK)
    shift = 1
    while shift < BLOCK:
        cum = cum + jnp.where(lane >= shift, pltpu.roll(cum, shift, 1), 0.0)
        shift *= 2
    cum_s[...] = cum
    last = cum[:, BLOCK - 1 : BLOCK] + cum[:, 2 * BLOCK - 1 : 2 * BLOCK]
    mine_s[...] = jnp.broadcast_to(last, mine_s.shape)

    @pl.when(z == 0)
    def _():
        fin_s[0] = jnp.zeros_like(fin_s[0])

    @pl.when(z == nz - 1)
    def _():
        fin_s[1] = jnp.zeros_like(fin_s[1])

    pl.semaphore_wait(barrier, n - 1 + nd - 1)
    decay_copy = pltpu.make_async_remote_copy(
        src_ref=mine_s, dst_ref=theirs_s, send_sem=dec_sem.at[0], recv_sem=dec_sem.at[1],
        device_id=(partner, d), device_id_type=MESH,
    )
    decay_copy.start()
    for copy in loads:
        copy.wait()
    decay_copy.wait()

    def cols(h):
        return pl.ds(pl.multiple_of(h * width, width), width)

    def blk(b):
        return pl.ds(b * BLOCK, BLOCK)

    def first_pass(h):
        c = cols(h)
        pre = mm(k_s[:, c], km_ref[h])
        sig = sigmoid(pre)
        sk_s[:, c] = sig * (1.0 + pre * (1.0 - sig))
        kf = (pre * sig).astype(BF16)
        kf_s[:, c] = kf
        pre = mm(q_s[:, c], qm_ref[h])
        sig = sigmoid(pre)
        sq_s[:, c] = sig * (1.0 + pre * (1.0 - sig))
        qf = (pre * sig).astype(BF16)
        qf_s[:, c] = qf
        col = jnp.broadcast_to(cum_s[pl.ds(h, 1), :], (width, tokens)).T
        col_s[h] = col
        u, w = [], []
        for b in range(2):
            cb = col[b * BLOCK : (b + 1) * BLOCK]
            tot = cb[BLOCK - 1 : BLOCK]
            part = slice(b * BLOCK, (b + 1) * BLOCK)
            ek = jnp.exp(tot - cb)
            eq = jnp.exp(cb)
            ek_s[h, blk(b), :] = ek
            eq_s[h, blk(b), :] = eq
            kd = (kf[part].astype(F32) * ek).astype(BF16)
            kd_s[blk(b), c] = kd
            u.append(mm_tn(kd, v_s[blk(b), c]))
            qd = (qf[part].astype(F32) * eq).astype(BF16)
            qd_s[blk(b), c] = qd
            w.append(mm_tn(qd, g_s[blk(b), c]))
        d0 = jnp.exp(col[BLOCK - 1 : BLOCK])
        d1 = jnp.exp(col[2 * BLOCK - 1 : 2 * BLOCK])
        U_s[h] = d1 * u[0] + u[1]
        u0_s[h] = u[0]
        C_s[h] = w[0] + d0 * w[1]
        c1_s[h] = w[1]

    def chain_copy(way, h):
        to = z + 1 if way == 0 else z - 1
        to = jnp.clip(to, 0, nz - 1) * 2 + x
        return pltpu.make_async_remote_copy(
            src_ref=fout_s.at[way, h], dst_ref=fin_s.at[way, h],
            send_sem=ch_send.at[way, h], recv_sem=ch_recv.at[way, h],
            device_id=(to, d), device_id_type=MESH,
        )

    def cross_copy(way, h):
        return pltpu.make_async_remote_copy(
            src_ref=xout_s.at[way, h], dst_ref=xin_s.at[way, h],
            send_sem=x_send.at[way, h], recv_sem=x_recv.at[way, h],
            device_id=(partner, d), device_id_type=MESH,
        )

    def is_first(way):
        return (x == 0) if way == 0 else (x == 1)

    def has_in(way):
        return (z > 0) if way == 0 else (z < nz - 1)

    def has_out(way):
        return (z < nz - 1) if way == 0 else (z > 0)

    def chain(way, h):
        @pl.when(has_in(way))
        def _():
            chain_copy(way, h).wait_recv()

        own = mine_s[pl.ds(h, 1), :]
        other = theirs_s[pl.ds(h, 1), :]
        state = fin_s[way, h]
        term = (U_s if way == 0 else C_s)[h]
        first = is_first(way)

        @pl.when(has_out(way))
        def _():
            carry = jnp.where(first, jnp.exp(other), 1.0)
            fout_s[way, h] = jnp.exp(own + other) * state + carry * term
            chain_copy(way, h).start()

        keep = jnp.where(first, jnp.exp(own), 1.0)
        xout_s[way, h] = keep * state + jnp.where(first, term, 0.0)
        cross_copy(way, h).start()

    def entering(way, h):
        cross_copy(way, h).wait_recv()
        other = theirs_s[pl.ds(h, 1), :]
        keep = jnp.where(is_first(way), 1.0, jnp.exp(other))
        return keep * fin_s[way, h] + xin_s[way, h]

    def part_copy(m, r):
        to = lax.rem(d + r, nd)
        return pltpu.make_async_remote_copy(
            src_ref=part_s.at[to, m], dst_ref=pin_s.at[r - 1, m],
            send_sem=p_send.at[r - 1, m], recv_sem=p_recv.at[r - 1, m],
            device_id=(me, to), device_id_type=MESH,
        )

    def send_part(m, part):
        for i in range(nd):
            part_s[i, m] = part[i * rows : (i + 1) * rows]
        for r in range(1, nd):
            part_copy(m, r).start()

    half = BLOCK // 2
    iota0 = lax.broadcasted_iota(jnp.int32, (half, half), 0)
    iota1 = lax.broadcasted_iota(jnp.int32, (half, half), 1)
    low, high = slice(0, half), slice(half, BLOCK)

    def stack(a, b, axis):
        return jnp.concatenate([a, b], axis=axis)

    def masked_exp(keep, value):
        return jnp.exp(jnp.where(keep, value, -1e30))

    def finish_q(h):
        c = cols(h)
        state = entering(0, h)
        d0 = jnp.exp(col_s[h, pl.ds(BLOCK - 1, 1), :])
        states = (state.astype(BF16), (d0 * state + u0_s[h]).astype(BF16))
        total = None
        for b in range(2):
            st = states[b]
            cb = col_s[h, blk(b), :]
            row = cum_s[pl.ds(h, 1), blk(b)]
            w0 = masked_exp(iota0 >= iota1, cb[low] - row[:, low])
            w1 = stack(
                jnp.exp(cb[high] - row[:, low]),
                masked_exp(iota0 >= iota1, cb[high] - row[:, high]),
                1,
            )
            qf, kf, v, g = qf_s[blk(b), c], kf_s[blk(b), c], v_s[blk(b), c], g_s[blk(b), c]
            p0 = (mm_nt(qf[low], kf[low]) * w0).astype(BF16)
            p1 = (mm_nt(qf[high], kf) * w1).astype(BF16)
            intra = stack(mm(p0, v[low]), mm(p1, v), 0)
            o_s[blk(b), c] = (scale * (intra + mm(qd_s[blk(b), c], st))).astype(BF16)
            g0 = (mm_nt(g[low], v[low]) * w0).astype(BF16)
            g1 = (mm_nt(g[high], v) * w1).astype(BF16)
            intra = stack(mm(g0, kf[low]), mm(g1, kf), 0)
            gf = scale * (intra + eq_s[h, blk(b), :] * mm_nt(g, st))
            gp = (gf * sq_s[blk(b), c]).astype(BF16)
            gq_s[blk(b), c] = mm_nt(gp, qm_ref[h]).astype(BF16)
            p = mm_tn(q_s[blk(b), c], gp)
            total = p if total is None else total + p
        send_part((h // hh) * heads + lax.rem(h, hh), total)

    def finish_k(h):
        c = cols(h)
        after = entering(1, h)
        d1 = jnp.exp(col_s[h, pl.ds(2 * BLOCK - 1, 1), :])
        afters = ((c1_s[h] + d1 * after).astype(BF16), after.astype(BF16))
        total = None
        for b in range(2):
            af = afters[b]
            cb = col_s[h, blk(b), :]
            row = cum_s[pl.ds(h, 1), blk(b)]
            w0 = stack(
                masked_exp(iota1 >= iota0, row[:, low] - cb[low]),
                jnp.exp(row[:, high] - cb[low]),
                1,
            )
            w1 = masked_exp(iota1 >= iota0, row[:, high] - cb[high])
            qf, kf, v, g = qf_s[blk(b), c], kf_s[blk(b), c], v_s[blk(b), c], g_s[blk(b), c]
            p0 = (mm_nt(kf[low], qf) * w0).astype(BF16)
            p1 = (mm_nt(kf[high], qf[high]) * w1).astype(BF16)
            intra = stack(mm(p0, g), mm(p1, g[high]), 0)
            gv_s[blk(b), c] = (scale * (intra + mm(kd_s[blk(b), c], af))).astype(BF16)
            g0 = (mm_nt(v[low], g) * w0).astype(BF16)
            g1 = (mm_nt(v[high], g[high]) * w1).astype(BF16)
            intra = stack(mm(g0, qf), mm(g1, qf[high]), 0)
            gf = scale * (intra + ek_s[h, blk(b), :] * mm_nt(v, af))
            gp = (gf * sk_s[blk(b), c]).astype(BF16)
            gk_s[blk(b), c] = mm_nt(gp, km_ref[h]).astype(BF16)
            p = mm_tn(k_s[blk(b), c], gp)
            total = p if total is None else total + p
        send_part((h // hh) * heads + hh + lax.rem(h, hh), total)

    size = own_s.shape[0] // (groups * n)

    def piece(t, i):
        return pl.ds(pl.multiple_of((t * n + i) * size, size), size)

    def back(r):
        return lax.rem(me + n - r, n)

    def ctx_copy(t, r):
        to = lax.rem(me + r, n)
        return pltpu.make_async_remote_copy(
            src_ref=own_s.at[piece(t, to)], dst_ref=cin_s.at[t, r - 1],
            send_sem=c_send.at[t, r - 1], recv_sem=c_recv.at[t, r - 1],
            device_id=(to, d), device_id_type=MESH,
        )

    def gather_copy(t, r, i):
        return pltpu.make_async_remote_copy(
            src_ref=res_s.at[d, piece(t, i)], dst_ref=res_s.at[d, piece(t, i)],
            send_sem=ag_send.at[t, r - 1], recv_sem=ag_recv.at[t, r - 1],
            device_id=(lax.rem(me + r, n), d), device_id_type=MESH,
        )

    across = lax.rem(d + 2, nd)
    beside = d + 1 - 2 * lax.rem(d, 2)
    diagonal = lax.rem(beside + 2, nd)

    def y_copy(t, r, whose):
        at = piece(t, back(r))
        return pltpu.make_async_remote_copy(
            src_ref=res_s.at[whose, at], dst_ref=res_s.at[whose, at],
            send_sem=y_send.at[t, r], recv_sem=y_recv.at[t, r],
            device_id=(me, across), device_id_type=MESH,
        )

    def core_copy(t, r, i, whose):
        at = piece(t, back(r))
        return pltpu.make_async_remote_copy(
            src_ref=res_s.at[whose, at], dst_ref=res_s.at[whose, at],
            send_sem=k_send.at[t, i, r], recv_sem=k_recv.at[t, i, r],
            device_id=(me, beside), device_id_type=MESH,
        )

    def reduce_dp(t):
        @pl.loop(0, 2 * hh)
        def _(i):
            m = t * 2 * hh + i
            total = part_s[d, m]
            for r in range(1, nd):
                part_copy(m, r).wait_recv()
                total = total + pin_s[r - 1, m]
            own_s[pl.ds(pl.multiple_of(m * rows, rows), rows), :] = total

        @pl.loop(1, n)
        def _(r):
            ctx_copy(t, r).start()

    def reduce_ctx(t):
        res_s[d, piece(t, me)] = own_s[piece(t, me)]

        @pl.loop(1, n)
        def _(r):
            ctx_copy(t, r).wait_recv()
            res_s[d, piece(t, me)] = res_s[d, piece(t, me)] + cin_s[t, r - 1]

        @pl.loop(1, n)
        def _(r):
            gather_copy(t, r, me).start()

        y_copy(t, 0, d).start()
        core_copy(t, 0, 0, d).start()

    def gather_ctx(t):
        @pl.loop(1, n)
        def _(r):
            gather_copy(t, r, back(r)).wait_recv()
            y_copy(t, r, d).start()
            core_copy(t, r, 0, d).start()

    def gather_y(t):
        @pl.loop(0, n)
        def _(r):
            y_copy(t, r, across).wait_recv()
            core_copy(t, r, 1, across).start()

    def gather_core(t):
        @pl.loop(0, n)
        def _(r):
            core_copy(t, r, 0, beside).wait_recv()
            core_copy(t, r, 1, diagonal).wait_recv()

    stages = (reduce_dp, reduce_ctx, gather_ctx, gather_y)
    steps = heads + 2 * (nz - 1) + 2
    ready = hh + 2 * (nz - 1) + 2

    def inside(h):
        return jnp.logical_and(h >= 0, h < heads)

    @pl.loop(0, steps)
    def _(s):
        hf = s - 2 * z
        ha = s - 2 * (nz - 1 - z)

        @pl.when(s < heads)
        def _():
            first_pass(s)

        @pl.when(inside(hf))
        def _():
            chain(0, hf)

        @pl.when(inside(ha))
        def _():
            chain(1, ha)

        @pl.when(inside(hf - 2))
        def _():
            finish_q(hf - 2)

        @pl.when(inside(ha - 2))
        def _():
            finish_k(ha - 2)

        if groups == 2:
            for i, stage in enumerate(stages):
                pl.when(s == ready + i)(functools.partial(stage, 0))

    stores = [
        pltpu.make_async_copy(src, dst, out_sem.at[i])
        for i, (src, dst) in enumerate(((o_s, o_h), (gq_s, gq_h), (gk_s, gk_h), (gv_s, gv_h)))
    ]
    for copy in stores:
        copy.start()
    for stage in stages:
        stage(groups - 1)
    for t in range(groups):
        gather_core(t)

    result = pltpu.make_async_copy(res_s, res_h, out_sem.at[4])
    result.start()

    @pl.loop(0, heads)
    def _(h):
        for way in range(2):
            cross_copy(way, h).wait_send()

            @pl.when(has_out(way))
            def _():
                chain_copy(way, h).wait_send()

    @pl.loop(0, 2 * heads)
    def _(m):
        for r in range(1, nd):
            part_copy(m, r).wait_send()

    for t in range(groups):

        @pl.loop(1, n)
        def _(r):
            ctx_copy(t, r).wait_send()
            gather_copy(t, r, me).wait_send()

        @pl.loop(0, n)
        def _(r):
            y_copy(t, r, d).wait_send()
            core_copy(t, r, 0, d).wait_send()
            core_copy(t, r, 1, across).wait_send()

    for copy in stores:
        copy.wait()
    result.wait()


def place(nd, groups, hh, rows, a0, a1, a2, a3, maps, b0, b1, b2, b3, qm, km, sem, map_sem):
    copies = [
        pltpu.make_async_copy(src, dst, sem.at[i])
        for i, (src, dst) in enumerate(((a0, b0), (a1, b1), (a2, b2), (a3, b3)))
    ]
    for i in range(nd):
        for t in range(groups):
            for w, dst in enumerate((qm, km)):
                copies.append(
                    pltpu.make_async_copy(
                        maps.at[i, pl.ds((2 * t + w) * hh, hh)],
                        dst.at[pl.ds(t * hh, hh), pl.ds(i * rows, rows)],
                        map_sem.at[i, t, w],
                    )
                )
    for copy in copies:
        copy.start()
    for copy in copies:
        copy.wait()


def solution(mesh):
    n, nd = mesh.shape["ctx"], mesh.shape["dp"]

    def local(query, key, value, log_decay, grad_out, query_map, key_map):
        heads, width = query_map.shape[0], query_map.shape[1]
        tokens = query.shape[1]
        wide = heads * width
        rows = width // nd
        owned = 2 * heads * rows
        groups = 2 if owned % (2 * 8 * n) == 0 else 1
        hh = heads // groups
        any_spec = pl.BlockSpec(memory_space=pl.ANY)
        vmem_spec = pl.BlockSpec(memory_space=pltpu.VMEM)
        act = pltpu.VMEM((tokens, wide), BF16)
        act32 = pltpu.VMEM((tokens, wide), F32)
        mats = pltpu.VMEM((heads, width, width), F32)
        mats2 = pltpu.VMEM((2, heads, width, width), F32)
        dma = pltpu.SemaphoreType.DMA
        outs = pl.pallas_call(
            functools.partial(kernel, n, nd, groups, heads, width, tokens),
            out_shape=[jax.ShapeDtypeStruct((tokens, wide), BF16)] * 4
            + [jax.ShapeDtypeStruct((nd, owned, width), F32)],
            in_specs=[any_spec, any_spec, any_spec, vmem_spec, any_spec, vmem_spec, vmem_spec],
            out_specs=[any_spec] * 5,
            scratch_shapes=[act] * 8
            + [act32] * 2
            + [act] * 4
            + [
                pltpu.VMEM((heads, tokens), F32),
                pltpu.VMEM((heads, tokens, width), F32),
                pltpu.VMEM((heads, tokens, width), F32),
                pltpu.VMEM((heads, tokens, width), F32),
                pltpu.VMEM((heads, width), F32),
                pltpu.VMEM((heads, width), F32),
            ]
            + [mats] * 4
            + [mats2] * 4
            + [
                pltpu.VMEM((nd, 2 * heads, rows, width), F32),
                pltpu.VMEM((nd - 1, 2 * heads, rows, width), F32),
                pltpu.VMEM((owned, width), F32),
                pltpu.VMEM((groups, n - 1, owned // (groups * n), width), F32),
                pltpu.VMEM((nd, owned, width), F32),
            ]
            + [
                dma((4,)),
                dma((5,)),
                dma((2,)),
                dma((2, heads)),
                dma((2, heads)),
                dma((2, heads)),
                dma((2, heads)),
                dma((nd - 1, 2 * heads)),
                dma((nd - 1, 2 * heads)),
                dma((groups, n - 1)),
                dma((groups, n - 1)),
                dma((groups, n - 1)),
                dma((groups, n - 1)),
                dma((groups, n)),
                dma((groups, n)),
                dma((groups, 2, n)),
                dma((groups, 2, n)),
            ],
            compiler_params=pltpu.CompilerParams(
                collective_id=0, has_side_effects=True, vmem_limit_bytes=60 * 1024 * 1024
            ),
            cost_estimate=pl.CostEstimate(
                flops=4_000_000_000, bytes_accessed=10_000_000, transcendentals=4_000_000
            ),
        )(query[0], key[0], value[0], log_decay[0], grad_out[0], query_map, key_map)
        maps = outs[4].reshape(nd, 2 * heads, rows, width)
        final = pl.pallas_call(
            functools.partial(place, nd, groups, hh, rows),
            out_shape=[jax.ShapeDtypeStruct((tokens, wide), BF16)] * 4
            + [jax.ShapeDtypeStruct((heads, width, width), F32)] * 2,
            in_specs=[any_spec] * 5,
            out_specs=[any_spec] * 6,
            scratch_shapes=[dma((4,)), dma((nd, groups, 2))],
            compiler_params=pltpu.CompilerParams(vmem_limit_bytes=60 * 1024 * 1024),
        )(*outs[:4], maps)
        return tuple(a[None] for a in final[:4]) + tuple(final[4:])

    return jax.shard_map(
        local,
        mesh=mesh,
        in_specs=(
            P("dp", "ctx", None),
            P("dp", "ctx", None),
            P("dp", "ctx", None),
            P("dp", None, "ctx"),
            P("dp", "ctx", None),
            P(),
            P(),
        ),
        out_specs=(
            P("dp", "ctx", None),
            P("dp", "ctx", None),
            P("dp", "ctx", None),
            P("dp", "ctx", None),
            P(),
            P(),
        ),
        check_vma=False,
    )
```

```python
import functools
import math

import jax
import jax.numpy as jnp
from jax import lax
from jax.experimental import pallas as pl
from jax.experimental.pallas import tpu as pltpu
from jax.sharding import PartitionSpec as P

BLOCK = 256
MESH = pl.DeviceIdType.MESH
F32 = jnp.float32
BF16 = jnp.bfloat16


def mm(a, b):
    return lax.dot_general(a, b, (((1,), (0,)), ((), ())), preferred_element_type=F32)


def mm_nt(a, b):
    return lax.dot_general(a, b, (((1,), (1,)), ((), ())), preferred_element_type=F32)


def mm_tn(a, b):
    return lax.dot_general(a, b, (((0,), (0,)), ((), ())), preferred_element_type=F32)


def sigmoid(u):
    return 1.0 / (1.0 + jnp.exp(-u))


def kernel(
    n, nd, groups, heads, width, tokens,
    q_h, k_h, v_h, ld_ref, g_h, qm_ref, km_ref,
    o_h, gq_h, gk_h, gv_h, res_h,
    q_s, k_s, v_s, g_s, o_s, gq_s, gk_s, gv_s,
    sq_s, sk_s, qf_s, kf_s, qd_s, kd_s,
    cum_s, col_s, eq_s, ek_s, mine_s, theirs_s,
    U_s, C_s, u0_s, c1_s, fin_s, fout_s, xout_s, xin_s,
    part_s, pin_s, own_s, cin_s, res_s,
    in_sem, out_sem, dec_sem, ch_send, ch_recv, x_send, x_recv,
    p_send, p_recv, c_send, c_recv, ag_send, ag_recv,
    y_send, y_recv, k_send, k_recv,
):
    scale = 1.0 / (width * math.sqrt(BLOCK))
    me = lax.axis_index("ctx")
    d = lax.axis_index("dp")
    nz = n // 2
    z = me // 2
    x = lax.rem(me, 2)
    partner = me + 1 - 2 * x
    rows = width // nd
    hh = heads // groups

    loads = [
        pltpu.make_async_copy(src, dst, in_sem.at[i])
        for i, (src, dst) in enumerate(((k_h, k_s), (v_h, v_s), (q_h, q_s), (g_h, g_s)))
    ]
    for copy in loads:
        copy.start()

    barrier = pltpu.get_barrier_semaphore()

    @pl.loop(1, n)
    def _(r):
        pl.semaphore_signal(
            barrier, inc=1, device_id=(lax.rem(me + r, n), d), device_id_type=MESH
        )

    for r in range(1, nd):
        pl.semaphore_signal(
            barrier, inc=1, device_id=(me, lax.rem(d + r, nd)), device_id_type=MESH
        )

    cum = ld_ref[...]
    lane = lax.rem(lax.broadcasted_iota(jnp.int32, cum.shape, 1), BLOCK)
    shift = 1
    while shift < BLOCK:
        cum = cum + jnp.where(lane >= shift, pltpu.roll(cum, shift, 1), 0.0)
        shift *= 2
    cum_s[...] = cum
    last = cum[:, BLOCK - 1 : BLOCK] + cum[:, 2 * BLOCK - 1 : 2 * BLOCK]
    mine_s[...] = jnp.broadcast_to(last, mine_s.shape)

    @pl.when(z == 0)
    def _():
        fin_s[0] = jnp.zeros_like(fin_s[0])

    @pl.when(z == nz - 1)
    def _():
        fin_s[1] = jnp.zeros_like(fin_s[1])

    pl.semaphore_wait(barrier, n - 1 + nd - 1)
    decay_copy = pltpu.make_async_remote_copy(
        src_ref=mine_s, dst_ref=theirs_s, send_sem=dec_sem.at[0], recv_sem=dec_sem.at[1],
        device_id=(partner, d), device_id_type=MESH,
    )
    decay_copy.start()
    for copy in loads:
        copy.wait()
    decay_copy.wait()

    def cols(h):
        return pl.ds(pl.multiple_of(h * width, width), width)

    def blk(b):
        return pl.ds(b * BLOCK, BLOCK)

    def first_pass(h):
        c = cols(h)
        pre = mm(k_s[:, c], km_ref[h])
        sig = sigmoid(pre)
        sk_s[:, c] = sig * (1.0 + pre * (1.0 - sig))
        kf = (pre * sig).astype(BF16)
        kf_s[:, c] = kf
        pre = mm(q_s[:, c], qm_ref[h])
        sig = sigmoid(pre)
        sq_s[:, c] = sig * (1.0 + pre * (1.0 - sig))
        qf = (pre * sig).astype(BF16)
        qf_s[:, c] = qf
        col = jnp.broadcast_to(cum_s[pl.ds(h, 1), :], (width, tokens)).T
        col_s[h] = col
        u, w = [], []
        for b in range(2):
            cb = col[b * BLOCK : (b + 1) * BLOCK]
            tot = cb[BLOCK - 1 : BLOCK]
            part = slice(b * BLOCK, (b + 1) * BLOCK)
            ek = jnp.exp(tot - cb)
            eq = jnp.exp(cb)
            ek_s[h, blk(b), :] = ek
            eq_s[h, blk(b), :] = eq
            kd = (kf[part].astype(F32) * ek).astype(BF16)
            kd_s[blk(b), c] = kd
            u.append(mm_tn(kd, v_s[blk(b), c]))
            qd = (qf[part].astype(F32) * eq).astype(BF16)
            qd_s[blk(b), c] = qd
            w.append(mm_tn(qd, g_s[blk(b), c]))
        d0 = jnp.exp(col[BLOCK - 1 : BLOCK])
        d1 = jnp.exp(col[2 * BLOCK - 1 : 2 * BLOCK])
        U_s[h] = d1 * u[0] + u[1]
        u0_s[h] = u[0]
        C_s[h] = w[0] + d0 * w[1]
        c1_s[h] = w[1]

    def chain_copy(way, p):
        to = z + 1 if way == 0 else z - 1
        to = jnp.clip(to, 0, nz - 1) * 2 + x
        at = pl.ds(2 * p, 2)
        return pltpu.make_async_remote_copy(
            src_ref=fout_s.at[way, at], dst_ref=fin_s.at[way, at],
            send_sem=ch_send.at[way, p], recv_sem=ch_recv.at[way, p],
            device_id=(to, d), device_id_type=MESH,
        )

    def cross_copy(way, p):
        at = pl.ds(2 * p, 2)
        return pltpu.make_async_remote_copy(
            src_ref=xout_s.at[way, at], dst_ref=xin_s.at[way, at],
            send_sem=x_send.at[way, p], recv_sem=x_recv.at[way, p],
            device_id=(partner, d), device_id_type=MESH,
        )

    def is_first(way):
        return (x == 0) if way == 0 else (x == 1)

    def has_in(way):
        return (z > 0) if way == 0 else (z < nz - 1)

    def has_out(way):
        return (z < nz - 1) if way == 0 else (z > 0)

    def chain(way, p):
        @pl.when(has_in(way))
        def _():
            chain_copy(way, p).wait_recv()

        first = is_first(way)
        source = U_s if way == 0 else C_s

        @pl.when(has_out(way))
        def _():
            for h in (2 * p, 2 * p + 1):
                own = mine_s[pl.ds(h, 1), :]
                other = theirs_s[pl.ds(h, 1), :]
                carry = jnp.where(first, jnp.exp(other), 1.0)
                fout_s[way, h] = jnp.exp(own + other) * fin_s[way, h] + carry * source[h]
            chain_copy(way, p).start()

        for h in (2 * p, 2 * p + 1):
            keep = jnp.where(first, jnp.exp(mine_s[pl.ds(h, 1), :]), 1.0)
            xout_s[way, h] = keep * fin_s[way, h] + jnp.where(first, source[h], 0.0)
        cross_copy(way, p).start()

    def entering(way, h):
        other = theirs_s[pl.ds(h, 1), :]
        keep = jnp.where(is_first(way), 1.0, jnp.exp(other))
        return keep * fin_s[way, h] + xin_s[way, h]

    def part_copy(i, r):
        to = lax.rem(d + r, nd)
        at = pl.ds(2 * i, 2)
        return pltpu.make_async_remote_copy(
            src_ref=part_s.at[to, at], dst_ref=pin_s.at[r - 1, at],
            send_sem=p_send.at[r - 1, i], recv_sem=p_recv.at[r - 1, i],
            device_id=(me, to), device_id_type=MESH,
        )

    def keep_part(m, part):
        for i in range(nd):
            part_s[i, m] = part[i * rows : (i + 1) * rows]

    def send_parts(i):
        for r in range(1, nd):
            part_copy(i, r).start()

    half = BLOCK // 2
    iota0 = lax.broadcasted_iota(jnp.int32, (half, half), 0)
    iota1 = lax.broadcasted_iota(jnp.int32, (half, half), 1)
    low, high = slice(0, half), slice(half, BLOCK)

    def stack(a, b, axis):
        return jnp.concatenate([a, b], axis=axis)

    def masked_exp(keep, value):
        return jnp.exp(jnp.where(keep, value, -1e30))

    def finish_q(h):
        c = cols(h)
        state = entering(0, h)
        d0 = jnp.exp(col_s[h, pl.ds(BLOCK - 1, 1), :])
        states = (state.astype(BF16), (d0 * state + u0_s[h]).astype(BF16))
        total = None
        for b in range(2):
            st = states[b]
            cb = col_s[h, blk(b), :]
            row = cum_s[pl.ds(h, 1), blk(b)]
            w0 = masked_exp(iota0 >= iota1, cb[low] - row[:, low])
            w1 = stack(
                jnp.exp(cb[high] - row[:, low]),
                masked_exp(iota0 >= iota1, cb[high] - row[:, high]),
                1,
            )
            qf, kf, v, g = qf_s[blk(b), c], kf_s[blk(b), c], v_s[blk(b), c], g_s[blk(b), c]
            p0 = (mm_nt(qf[low], kf[low]) * w0).astype(BF16)
            p1 = (mm_nt(qf[high], kf) * w1).astype(BF16)
            intra = stack(mm(p0, v[low]), mm(p1, v), 0)
            o_s[blk(b), c] = (scale * (intra + mm(qd_s[blk(b), c], st))).astype(BF16)
            g0 = (mm_nt(g[low], v[low]) * w0).astype(BF16)
            g1 = (mm_nt(g[high], v) * w1).astype(BF16)
            intra = stack(mm(g0, kf[low]), mm(g1, kf), 0)
            gf = scale * (intra + eq_s[h, blk(b), :] * mm_nt(g, st))
            gp = (gf * sq_s[blk(b), c]).astype(BF16)
            gq_s[blk(b), c] = mm_nt(gp, qm_ref[h]).astype(BF16)
            p = mm_tn(q_s[blk(b), c], gp)
            total = p if total is None else total + p
        keep_part((h // hh) * heads + lax.rem(h, hh), total)

    def finish_k(h):
        c = cols(h)
        after = entering(1, h)
        d1 = jnp.exp(col_s[h, pl.ds(2 * BLOCK - 1, 1), :])
        afters = ((c1_s[h] + d1 * after).astype(BF16), after.astype(BF16))
        total = None
        for b in range(2):
            af = afters[b]
            cb = col_s[h, blk(b), :]
            row = cum_s[pl.ds(h, 1), blk(b)]
            w0 = stack(
                masked_exp(iota1 >= iota0, row[:, low] - cb[low]),
                jnp.exp(row[:, high] - cb[low]),
                1,
            )
            w1 = masked_exp(iota1 >= iota0, row[:, high] - cb[high])
            qf, kf, v, g = qf_s[blk(b), c], kf_s[blk(b), c], v_s[blk(b), c], g_s[blk(b), c]
            p0 = (mm_nt(kf[low], qf) * w0).astype(BF16)
            p1 = (mm_nt(kf[high], qf[high]) * w1).astype(BF16)
            intra = stack(mm(p0, g), mm(p1, g[high]), 0)
            gv_s[blk(b), c] = (scale * (intra + mm(kd_s[blk(b), c], af))).astype(BF16)
            g0 = (mm_nt(v[low], g) * w0).astype(BF16)
            g1 = (mm_nt(v[high], g[high]) * w1).astype(BF16)
            intra = stack(mm(g0, qf), mm(g1, qf[high]), 0)
            gf = scale * (intra + ek_s[h, blk(b), :] * mm_nt(v, af))
            gp = (gf * sk_s[blk(b), c]).astype(BF16)
            gk_s[blk(b), c] = mm_nt(gp, km_ref[h]).astype(BF16)
            p = mm_tn(k_s[blk(b), c], gp)
            total = p if total is None else total + p
        keep_part((h // hh) * heads + hh + lax.rem(h, hh), total)

    def first_passes(p):
        first_pass(2 * p)
        first_pass(2 * p + 1)

    def finish(way, p):
        cross_copy(way, p).wait_recv()
        for h in (2 * p, 2 * p + 1):
            (finish_q if way == 0 else finish_k)(h)
        hp = hh // 2
        send_parts((p // hp) * (heads // 2) + way * hp + lax.rem(p, hp))

    size = own_s.shape[0] // (groups * n)

    def piece(t, i):
        return pl.ds(pl.multiple_of((t * n + i) * size, size), size)

    def back(r):
        return lax.rem(me + n - r, n)

    def ctx_copy(t, r):
        to = lax.rem(me + r, n)
        return pltpu.make_async_remote_copy(
            src_ref=own_s.at[piece(t, to)], dst_ref=cin_s.at[t, r - 1],
            send_sem=c_send.at[t, r - 1], recv_sem=c_recv.at[t, r - 1],
            device_id=(to, d), device_id_type=MESH,
        )

    def gather_copy(t, r, i):
        return pltpu.make_async_remote_copy(
            src_ref=res_s.at[d, piece(t, i)], dst_ref=res_s.at[d, piece(t, i)],
            send_sem=ag_send.at[t, r - 1], recv_sem=ag_recv.at[t, r - 1],
            device_id=(lax.rem(me + r, n), d), device_id_type=MESH,
        )

    across = lax.rem(d + 2, nd)
    beside = d + 1 - 2 * lax.rem(d, 2)
    diagonal = lax.rem(beside + 2, nd)

    def y_copy(t, r, whose):
        at = piece(t, back(r))
        return pltpu.make_async_remote_copy(
            src_ref=res_s.at[whose, at], dst_ref=res_s.at[whose, at],
            send_sem=y_send.at[t, r], recv_sem=y_recv.at[t, r],
            device_id=(me, across), device_id_type=MESH,
        )

    def core_copy(t, r, i, whose):
        at = piece(t, back(r))
        return pltpu.make_async_remote_copy(
            src_ref=res_s.at[whose, at], dst_ref=res_s.at[whose, at],
            send_sem=k_send.at[t, i, r], recv_sem=k_recv.at[t, i, r],
            device_id=(me, beside), device_id_type=MESH,
        )

    def reduce_dp(t):
        @pl.loop(0, hh)
        def _(j):
            i = t * hh + j
            at = pl.ds(2 * i, 2)
            total = part_s[d, at]
            for r in range(1, nd):
                part_copy(i, r).wait_recv()
                total = total + pin_s[r - 1, at]
            span = pl.ds(pl.multiple_of(2 * i * rows, 2 * rows), 2 * rows)
            own_s[span, :] = total.reshape(2 * rows, width)

        @pl.loop(1, n)
        def _(r):
            ctx_copy(t, r).start()

    def reduce_ctx(t):
        res_s[d, piece(t, me)] = own_s[piece(t, me)]

        @pl.loop(1, n)
        def _(r):
            ctx_copy(t, r).wait_recv()
            res_s[d, piece(t, me)] = res_s[d, piece(t, me)] + cin_s[t, r - 1]

        @pl.loop(1, n)
        def _(r):
            gather_copy(t, r, me).start()

        y_copy(t, 0, d).start()
        core_copy(t, 0, 0, d).start()

    def gather_ctx(t):
        @pl.loop(1, n)
        def _(r):
            gather_copy(t, r, back(r)).wait_recv()
            y_copy(t, r, d).start()
            core_copy(t, r, 0, d).start()

    def gather_y(t):
        @pl.loop(0, n)
        def _(r):
            y_copy(t, r, across).wait_recv()
            core_copy(t, r, 1, across).start()

    def gather_core(t):
        @pl.loop(0, n)
        def _(r):
            core_copy(t, r, 0, beside).wait_recv()
            core_copy(t, r, 1, diagonal).wait_recv()

    stages = (reduce_dp, reduce_ctx, gather_ctx, gather_y)
    pairs = heads // 2
    steps = pairs + nz + 1
    ready = hh // 2 + nz + 1

    def inside(p):
        return jnp.logical_and(p >= 0, p < pairs)

    @pl.loop(0, steps)
    def _(s):
        pf = s - 1 - z
        pa = s - 1 - (nz - 1 - z)

        @pl.when(inside(pf))
        def _():
            chain(0, pf)

        @pl.when(inside(pa))
        def _():
            chain(1, pa)

        @pl.when(s < pairs)
        def _():
            first_passes(s)

        @pl.when(inside(pf - 1))
        def _():
            finish(0, pf - 1)

        @pl.when(inside(pa - 1))
        def _():
            finish(1, pa - 1)

        if groups == 2:
            for i, stage in enumerate(stages[:2]):
                pl.when(s == ready + i)(functools.partial(stage, 0))

    stores = [
        pltpu.make_async_copy(src, dst, out_sem.at[i])
        for i, (src, dst) in enumerate(((o_s, o_h), (gq_s, gq_h), (gk_s, gk_h), (gv_s, gv_h)))
    ]
    for copy in stores:
        copy.start()
    if groups == 2:
        reduce_dp(1)
        gather_ctx(0)
        reduce_ctx(1)
        gather_y(0)
        gather_ctx(1)
        gather_y(1)
    else:
        for stage in stages:
            stage(0)
    for t in range(groups):
        gather_core(t)

    result = pltpu.make_async_copy(res_s, res_h, out_sem.at[4])
    result.start()

    @pl.loop(0, pairs)
    def _(p):
        for way in range(2):
            cross_copy(way, p).wait_send()

            @pl.when(has_out(way))
            def _():
                chain_copy(way, p).wait_send()

    @pl.loop(0, heads)
    def _(i):
        for r in range(1, nd):
            part_copy(i, r).wait_send()

    for t in range(groups):

        @pl.loop(1, n)
        def _(r):
            ctx_copy(t, r).wait_send()
            gather_copy(t, r, me).wait_send()

        @pl.loop(0, n)
        def _(r):
            y_copy(t, r, d).wait_send()
            core_copy(t, r, 0, d).wait_send()
            core_copy(t, r, 1, across).wait_send()

    for copy in stores:
        copy.wait()
    result.wait()


def place(nd, groups, hh, rows, a0, a1, a2, a3, maps, b0, b1, b2, b3, qm, km, held, mats, sem, map_sem):
    pairs = ((a0, b0), (a1, b1), (a2, b2), (a3, b3))
    loads = [pltpu.make_async_copy(maps, mats, sem.at[0, 4])]
    loads += [pltpu.make_async_copy(src, held.at[i], sem.at[0, i]) for i, (src, _) in enumerate(pairs)]
    for copy in loads:
        copy.start()
    stores = []
    for i in range(nd):
        for t in range(groups):
            for w, dst in enumerate((qm, km)):
                stores.append(
                    pltpu.make_async_copy(
                        mats.at[i, pl.ds((2 * t + w) * hh, hh)],
                        dst.at[pl.ds(t * hh, hh), pl.ds(i * rows, rows)],
                        map_sem.at[i, t, w],
                    )
                )
    loads[0].wait()
    for copy in stores:
        copy.start()
    for i, (_, dst) in enumerate(pairs):
        loads[1 + i].wait()
        copy = pltpu.make_async_copy(held.at[i], dst, sem.at[1, i])
        copy.start()
        stores.append(copy)
    for copy in stores:
        copy.wait()


def solution(mesh):
    n, nd = mesh.shape["ctx"], mesh.shape["dp"]

    def local(query, key, value, log_decay, grad_out, query_map, key_map):
        heads, width = query_map.shape[0], query_map.shape[1]
        tokens = query.shape[1]
        wide = heads * width
        rows = width // nd
        owned = 2 * heads * rows
        groups = 2 if owned % (2 * 8 * n) == 0 else 1
        hh = heads // groups
        any_spec = pl.BlockSpec(memory_space=pl.ANY)
        vmem_spec = pl.BlockSpec(memory_space=pltpu.VMEM)
        act = pltpu.VMEM((tokens, wide), BF16)
        act32 = pltpu.VMEM((tokens, wide), F32)
        mats = pltpu.VMEM((heads, width, width), F32)
        mats2 = pltpu.VMEM((2, heads, width, width), F32)
        dma = pltpu.SemaphoreType.DMA
        outs = pl.pallas_call(
            functools.partial(kernel, n, nd, groups, heads, width, tokens),
            out_shape=[jax.ShapeDtypeStruct((tokens, wide), BF16)] * 4
            + [jax.ShapeDtypeStruct((nd, owned, width), F32)],
            in_specs=[any_spec, any_spec, any_spec, vmem_spec, any_spec, vmem_spec, vmem_spec],
            out_specs=[any_spec] * 5,
            scratch_shapes=[act] * 8
            + [act32] * 2
            + [act] * 4
            + [
                pltpu.VMEM((heads, tokens), F32),
                pltpu.VMEM((heads, tokens, width), F32),
                pltpu.VMEM((heads, tokens, width), F32),
                pltpu.VMEM((heads, tokens, width), F32),
                pltpu.VMEM((heads, width), F32),
                pltpu.VMEM((heads, width), F32),
            ]
            + [mats] * 4
            + [mats2] * 4
            + [
                pltpu.VMEM((nd, 2 * heads, rows, width), F32),
                pltpu.VMEM((nd - 1, 2 * heads, rows, width), F32),
                pltpu.VMEM((owned, width), F32),
                pltpu.VMEM((groups, n - 1, owned // (groups * n), width), F32),
                pltpu.VMEM((nd, owned, width), F32),
            ]
            + [
                dma((4,)),
                dma((5,)),
                dma((2,)),
                dma((2, heads // 2)),
                dma((2, heads // 2)),
                dma((2, heads // 2)),
                dma((2, heads // 2)),
                dma((nd - 1, heads)),
                dma((nd - 1, heads)),
                dma((groups, n - 1)),
                dma((groups, n - 1)),
                dma((groups, n - 1)),
                dma((groups, n - 1)),
                dma((groups, n)),
                dma((groups, n)),
                dma((groups, 2, n)),
                dma((groups, 2, n)),
            ],
            compiler_params=pltpu.CompilerParams(
                collective_id=0, has_side_effects=True, vmem_limit_bytes=60 * 1024 * 1024
            ),
            cost_estimate=pl.CostEstimate(
                flops=4_000_000_000, bytes_accessed=10_000_000, transcendentals=4_000_000
            ),
        )(query[0], key[0], value[0], log_decay[0], grad_out[0], query_map, key_map)
        maps = outs[4].reshape(nd, 2 * heads, rows, width)
        final = pl.pallas_call(
            functools.partial(place, nd, groups, hh, rows),
            out_shape=[jax.ShapeDtypeStruct((tokens, wide), BF16)] * 4
            + [jax.ShapeDtypeStruct((heads, width, width), F32)] * 2,
            in_specs=[any_spec] * 5,
            out_specs=[any_spec] * 6,
            scratch_shapes=[
                pltpu.VMEM((4, tokens, wide), BF16),
                pltpu.VMEM((nd, 2 * heads, rows, width), F32),
                dma((2, 5)),
                dma((nd, groups, 2)),
            ],
            compiler_params=pltpu.CompilerParams(vmem_limit_bytes=48 * 1024 * 1024),
        )(*outs[:4], maps)
        return tuple(a[None] for a in final[:4]) + tuple(final[4:])

    return jax.shard_map(
        local,
        mesh=mesh,
        in_specs=(
            P("dp", "ctx", None),
            P("dp", "ctx", None),
            P("dp", "ctx", None),
            P("dp", None, "ctx"),
            P("dp", "ctx", None),
            P(),
            P(),
        ),
        out_specs=(
            P("dp", "ctx", None),
            P("dp", "ctx", None),
            P("dp", "ctx", None),
            P("dp", "ctx", None),
            P(),
            P(),
        ),
        check_vma=False,
    )
```

```python
import functools
import math

import jax
import jax.numpy as jnp
from jax import lax
from jax.experimental import pallas as pl
from jax.experimental.pallas import tpu as pltpu
from jax.sharding import PartitionSpec as P

BLOCK = 256
MESH = pl.DeviceIdType.MESH
F32 = jnp.float32
BF16 = jnp.bfloat16


def mm(a, b):
    return lax.dot_general(a, b, (((1,), (0,)), ((), ())), preferred_element_type=F32)


def mm_nt(a, b):
    return lax.dot_general(a, b, (((1,), (1,)), ((), ())), preferred_element_type=F32)


def mm_tn(a, b):
    return lax.dot_general(a, b, (((0,), (0,)), ((), ())), preferred_element_type=F32)


def sigmoid(u):
    return 1.0 / (1.0 + jnp.exp(-u))


def kernel(
    n, nd, groups, heads, width, tokens,
    q_h, k_h, v_h, ld_ref, g_h, qm_ref, km_ref,
    o_h, gq_h, gk_h, gv_h, res_h,
    q_s, k_s, v_s, g_s, o_s, gq_s, gk_s, gv_s,
    sq_s, sk_s, qf_s, kf_s, qd_s, kd_s,
    cum_s, col_s, eq_s, ek_s, mine_s, theirs_s,
    U_s, C_s, u0_s, c1_s, fin_s, fout_s, xout_s, xin_s,
    part_s, pin_s, own_s, cin_s, res_s,
    in_sem, out_sem, dec_sem, ch_send, ch_recv, x_send, x_recv,
    p_send, p_recv, c_send, c_recv, ag_send, ag_recv,
    y_send, y_recv, k_send, k_recv,
):
    scale = 1.0 / (width * math.sqrt(BLOCK))
    me = lax.axis_index("ctx")
    d = lax.axis_index("dp")
    nz = n // 2
    z = me // 2
    x = lax.rem(me, 2)
    partner = me + 1 - 2 * x
    rows = width // nd
    hh = heads // groups

    loads = [
        pltpu.make_async_copy(src, dst, in_sem.at[i])
        for i, (src, dst) in enumerate(((k_h, k_s), (v_h, v_s), (q_h, q_s), (g_h, g_s)))
    ]
    for copy in loads:
        copy.start()

    barrier = pltpu.get_barrier_semaphore()

    @pl.loop(1, n)
    def _(r):
        pl.semaphore_signal(
            barrier, inc=1, device_id=(lax.rem(me + r, n), d), device_id_type=MESH
        )

    for r in range(1, nd):
        pl.semaphore_signal(
            barrier, inc=1, device_id=(me, lax.rem(d + r, nd)), device_id_type=MESH
        )

    cum = ld_ref[...]
    lane = lax.rem(lax.broadcasted_iota(jnp.int32, cum.shape, 1), BLOCK)
    shift = 1
    while shift < BLOCK:
        cum = cum + jnp.where(lane >= shift, pltpu.roll(cum, shift, 1), 0.0)
        shift *= 2
    cum_s[...] = cum
    last = cum[:, BLOCK - 1 : BLOCK] + cum[:, 2 * BLOCK - 1 : 2 * BLOCK]
    mine_s[...] = jnp.broadcast_to(last, mine_s.shape)

    @pl.when(z == 0)
    def _():
        fin_s[0] = jnp.zeros_like(fin_s[0])

    @pl.when(z == nz - 1)
    def _():
        fin_s[1] = jnp.zeros_like(fin_s[1])

    pl.semaphore_wait(barrier, n - 1 + nd - 1)
    decay_copy = pltpu.make_async_remote_copy(
        src_ref=mine_s, dst_ref=theirs_s, send_sem=dec_sem.at[0], recv_sem=dec_sem.at[1],
        device_id=(partner, d), device_id_type=MESH,
    )
    decay_copy.start()
    for copy in loads:
        copy.wait()

    def cols(h):
        return pl.ds(pl.multiple_of(h * width, width), width)

    def blk(b):
        return pl.ds(b * BLOCK, BLOCK)

    def first_pass(h):
        c = cols(h)
        pre = mm(k_s[:, c], km_ref[h])
        sig = sigmoid(pre)
        sk_s[:, c] = sig * (1.0 + pre * (1.0 - sig))
        kf = (pre * sig).astype(BF16)
        kf_s[:, c] = kf
        pre = mm(q_s[:, c], qm_ref[h])
        sig = sigmoid(pre)
        sq_s[:, c] = sig * (1.0 + pre * (1.0 - sig))
        qf = (pre * sig).astype(BF16)
        qf_s[:, c] = qf
        col = jnp.broadcast_to(cum_s[pl.ds(h, 1), :], (width, tokens)).T
        col_s[h] = col
        u, w = [], []
        for b in range(2):
            cb = col[b * BLOCK : (b + 1) * BLOCK]
            tot = cb[BLOCK - 1 : BLOCK]
            part = slice(b * BLOCK, (b + 1) * BLOCK)
            ek = jnp.exp(tot - cb)
            eq = jnp.exp(cb)
            ek_s[h, blk(b), :] = ek
            eq_s[h, blk(b), :] = eq
            kd = (kf[part].astype(F32) * ek).astype(BF16)
            kd_s[blk(b), c] = kd
            u.append(mm_tn(kd, v_s[blk(b), c]))
            qd = (qf[part].astype(F32) * eq).astype(BF16)
            qd_s[blk(b), c] = qd
            w.append(mm_tn(qd, g_s[blk(b), c]))
        d0 = jnp.exp(col[BLOCK - 1 : BLOCK])
        d1 = jnp.exp(col[2 * BLOCK - 1 : 2 * BLOCK])
        U_s[h] = d1 * u[0] + u[1]
        u0_s[h] = u[0]
        C_s[h] = w[0] + d0 * w[1]
        c1_s[h] = w[1]

    def chain_copy(way, p):
        to = z + 1 if way == 0 else z - 1
        to = jnp.clip(to, 0, nz - 1) * 2 + x
        at = pl.ds(2 * p, 2)
        return pltpu.make_async_remote_copy(
            src_ref=fout_s.at[way, at], dst_ref=fin_s.at[way, at],
            send_sem=ch_send.at[way, p], recv_sem=ch_recv.at[way, p],
            device_id=(to, d), device_id_type=MESH,
        )

    def cross_copy(way, p):
        at = pl.ds(2 * p, 2)
        return pltpu.make_async_remote_copy(
            src_ref=xout_s.at[way, at], dst_ref=xin_s.at[way, at],
            send_sem=x_send.at[way, p], recv_sem=x_recv.at[way, p],
            device_id=(partner, d), device_id_type=MESH,
        )

    def is_first(way):
        return (x == 0) if way == 0 else (x == 1)

    def has_in(way):
        return (z > 0) if way == 0 else (z < nz - 1)

    def has_out(way):
        return (z < nz - 1) if way == 0 else (z > 0)

    def chain(way, p):
        @pl.when(has_in(way))
        def _():
            chain_copy(way, p).wait_recv()

        first = is_first(way)
        source = U_s if way == 0 else C_s

        @pl.when(has_out(way))
        def _():
            for h in (2 * p, 2 * p + 1):
                own = mine_s[pl.ds(h, 1), :]
                other = theirs_s[pl.ds(h, 1), :]
                carry = jnp.where(first, jnp.exp(other), 1.0)
                fout_s[way, h] = jnp.exp(own + other) * fin_s[way, h] + carry * source[h]
            chain_copy(way, p).start()

        for h in (2 * p, 2 * p + 1):
            keep = jnp.where(first, jnp.exp(mine_s[pl.ds(h, 1), :]), 1.0)
            xout_s[way, h] = keep * fin_s[way, h] + jnp.where(first, source[h], 0.0)
        cross_copy(way, p).start()

    def entering(way, h):
        other = theirs_s[pl.ds(h, 1), :]
        keep = jnp.where(is_first(way), 1.0, jnp.exp(other))
        return keep * fin_s[way, h] + xin_s[way, h]

    def part_copy(i, r):
        to = lax.rem(d + r, nd)
        at = pl.ds(2 * i, 2)
        return pltpu.make_async_remote_copy(
            src_ref=part_s.at[to, at], dst_ref=pin_s.at[r - 1, at],
            send_sem=p_send.at[r - 1, i], recv_sem=p_recv.at[r - 1, i],
            device_id=(me, to), device_id_type=MESH,
        )

    def keep_part(m, part):
        for i in range(nd):
            part_s[i, m] = part[i * rows : (i + 1) * rows]

    def send_parts(i):
        for r in range(1, nd):
            part_copy(i, r).start()

    half = BLOCK // 2
    iota0 = lax.broadcasted_iota(jnp.int32, (half, half), 0)
    iota1 = lax.broadcasted_iota(jnp.int32, (half, half), 1)
    low, high = slice(0, half), slice(half, BLOCK)

    def stack(a, b, axis):
        return jnp.concatenate([a, b], axis=axis)

    def masked_exp(keep, value):
        return jnp.exp(jnp.where(keep, value, -1e30))

    def finish_q(h):
        c = cols(h)
        state = entering(0, h)
        d0 = jnp.exp(col_s[h, pl.ds(BLOCK - 1, 1), :])
        states = (state.astype(BF16), (d0 * state + u0_s[h]).astype(BF16))
        total = None
        for b in range(2):
            st = states[b]
            cb = col_s[h, blk(b), :]
            row = cum_s[pl.ds(h, 1), blk(b)]
            w0 = masked_exp(iota0 >= iota1, cb[low] - row[:, low])
            w1 = stack(
                jnp.exp(cb[high] - row[:, low]),
                masked_exp(iota0 >= iota1, cb[high] - row[:, high]),
                1,
            )
            qf, kf, v, g = qf_s[blk(b), c], kf_s[blk(b), c], v_s[blk(b), c], g_s[blk(b), c]
            p0 = (mm_nt(qf[low], kf[low]) * w0).astype(BF16)
            p1 = (mm_nt(qf[high], kf) * w1).astype(BF16)
            intra = stack(mm(p0, v[low]), mm(p1, v), 0)
            o_s[blk(b), c] = (scale * (intra + mm(qd_s[blk(b), c], st))).astype(BF16)
            g0 = (mm_nt(g[low], v[low]) * w0).astype(BF16)
            g1 = (mm_nt(g[high], v) * w1).astype(BF16)
            intra = stack(mm(g0, kf[low]), mm(g1, kf), 0)
            gf = scale * (intra + eq_s[h, blk(b), :] * mm_nt(g, st))
            gp = (gf * sq_s[blk(b), c]).astype(BF16)
            gq_s[blk(b), c] = mm_nt(gp, qm_ref[h]).astype(BF16)
            p = mm_tn(q_s[blk(b), c], gp)
            total = p if total is None else total + p
        keep_part((h // hh) * heads + lax.rem(h, hh), total)

    def finish_k(h):
        c = cols(h)
        after = entering(1, h)
        d1 = jnp.exp(col_s[h, pl.ds(2 * BLOCK - 1, 1), :])
        afters = ((c1_s[h] + d1 * after).astype(BF16), after.astype(BF16))
        total = None
        for b in range(2):
            af = afters[b]
            cb = col_s[h, blk(b), :]
            row = cum_s[pl.ds(h, 1), blk(b)]
            w0 = stack(
                masked_exp(iota1 >= iota0, row[:, low] - cb[low]),
                jnp.exp(row[:, high] - cb[low]),
                1,
            )
            w1 = masked_exp(iota1 >= iota0, row[:, high] - cb[high])
            qf, kf, v, g = qf_s[blk(b), c], kf_s[blk(b), c], v_s[blk(b), c], g_s[blk(b), c]
            p0 = (mm_nt(kf[low], qf) * w0).astype(BF16)
            p1 = (mm_nt(kf[high], qf[high]) * w1).astype(BF16)
            intra = stack(mm(p0, g), mm(p1, g[high]), 0)
            gv_s[blk(b), c] = (scale * (intra + mm(kd_s[blk(b), c], af))).astype(BF16)
            g0 = (mm_nt(v[low], g) * w0).astype(BF16)
            g1 = (mm_nt(v[high], g[high]) * w1).astype(BF16)
            intra = stack(mm(g0, qf), mm(g1, qf[high]), 0)
            gf = scale * (intra + ek_s[h, blk(b), :] * mm_nt(v, af))
            gp = (gf * sk_s[blk(b), c]).astype(BF16)
            gk_s[blk(b), c] = mm_nt(gp, km_ref[h]).astype(BF16)
            p = mm_tn(k_s[blk(b), c], gp)
            total = p if total is None else total + p
        keep_part((h // hh) * heads + hh + lax.rem(h, hh), total)

    def first_passes(p):
        first_pass(2 * p)
        first_pass(2 * p + 1)

    def finish(way, p):
        cross_copy(way, p).wait_recv()
        for h in (2 * p, 2 * p + 1):
            (finish_q if way == 0 else finish_k)(h)
        hp = hh // 2
        send_parts((p // hp) * (heads // 2) + way * hp + lax.rem(p, hp))

    size = own_s.shape[0] // (groups * n)

    def piece(t, i):
        return pl.ds(pl.multiple_of((t * n + i) * size, size), size)

    def back(r):
        return lax.rem(me + n - r, n)

    def ctx_copy(t, r):
        to = lax.rem(me + r, n)
        return pltpu.make_async_remote_copy(
            src_ref=own_s.at[piece(t, to)], dst_ref=cin_s.at[t, r - 1],
            send_sem=c_send.at[t, r - 1], recv_sem=c_recv.at[t, r - 1],
            device_id=(to, d), device_id_type=MESH,
        )

    def gather_copy(t, r, i):
        return pltpu.make_async_remote_copy(
            src_ref=res_s.at[d, piece(t, i)], dst_ref=res_s.at[d, piece(t, i)],
            send_sem=ag_send.at[t, r - 1], recv_sem=ag_recv.at[t, r - 1],
            device_id=(lax.rem(me + r, n), d), device_id_type=MESH,
        )

    across = lax.rem(d + 2, nd)
    beside = d + 1 - 2 * lax.rem(d, 2)
    diagonal = lax.rem(beside + 2, nd)

    def y_copy(t, r, whose):
        at = piece(t, back(r))
        return pltpu.make_async_remote_copy(
            src_ref=res_s.at[whose, at], dst_ref=res_s.at[whose, at],
            send_sem=y_send.at[t, r], recv_sem=y_recv.at[t, r],
            device_id=(me, across), device_id_type=MESH,
        )

    def core_copy(t, r, i, whose):
        at = piece(t, back(r))
        return pltpu.make_async_remote_copy(
            src_ref=res_s.at[whose, at], dst_ref=res_s.at[whose, at],
            send_sem=k_send.at[t, i, r], recv_sem=k_recv.at[t, i, r],
            device_id=(me, beside), device_id_type=MESH,
        )

    def reduce_dp(t):
        @pl.loop(0, hh)
        def _(j):
            i = t * hh + j
            at = pl.ds(2 * i, 2)
            total = part_s[d, at]
            for r in range(1, nd):
                part_copy(i, r).wait_recv()
                total = total + pin_s[r - 1, at]
            span = pl.ds(pl.multiple_of(2 * i * rows, 2 * rows), 2 * rows)
            own_s[span, :] = total.reshape(2 * rows, width)

        @pl.loop(1, n)
        def _(r):
            ctx_copy(t, r).start()

    def reduce_ctx(t):
        res_s[d, piece(t, me)] = own_s[piece(t, me)]

        @pl.loop(1, n)
        def _(r):
            ctx_copy(t, r).wait_recv()
            res_s[d, piece(t, me)] = res_s[d, piece(t, me)] + cin_s[t, r - 1]

        @pl.loop(1, n)
        def _(r):
            gather_copy(t, r, me).start()

        y_copy(t, 0, d).start()
        core_copy(t, 0, 0, d).start()

    def gather_ctx(t):
        @pl.loop(1, n)
        def _(r):
            gather_copy(t, r, back(r)).wait_recv()
            y_copy(t, r, d).start()
            core_copy(t, r, 0, d).start()

    def gather_y(t):
        @pl.loop(0, n)
        def _(r):
            y_copy(t, r, across).wait_recv()
            core_copy(t, r, 1, across).start()

    def gather_core(t):
        @pl.loop(0, n)
        def _(r):
            core_copy(t, r, 0, beside).wait_recv()
            core_copy(t, r, 1, diagonal).wait_recv()

    stages = (reduce_dp, reduce_ctx, gather_ctx, gather_y)
    pairs = heads // 2
    steps = pairs + nz + 1
    ready = hh // 2 + nz + 1

    def inside(p):
        return jnp.logical_and(p >= 0, p < pairs)

    @pl.loop(0, steps)
    def _(s):
        pf = s - 1 - z
        pa = s - 1 - (nz - 1 - z)

        @pl.when(s == 1)
        def _():
            decay_copy.wait()

        @pl.when(inside(pf))
        def _():
            chain(0, pf)

        @pl.when(inside(pa))
        def _():
            chain(1, pa)

        @pl.when(s < pairs)
        def _():
            first_passes(s)

        @pl.when(inside(pf - 1))
        def _():
            finish(0, pf - 1)

        @pl.when(inside(pa - 1))
        def _():
            finish(1, pa - 1)

        if groups == 2:
            for i, stage in enumerate(stages[:2]):
                pl.when(s == ready + i)(functools.partial(stage, 0))

    stores = [
        pltpu.make_async_copy(src, dst, out_sem.at[i])
        for i, (src, dst) in enumerate(((o_s, o_h), (gq_s, gq_h), (gk_s, gk_h), (gv_s, gv_h)))
    ]
    for copy in stores:
        copy.start()
    if groups == 2:
        reduce_dp(1)
        gather_ctx(0)
        reduce_ctx(1)
        gather_y(0)
        gather_ctx(1)
        gather_y(1)
    else:
        for stage in stages:
            stage(0)
    for t in range(groups):
        gather_core(t)

    result = pltpu.make_async_copy(res_s, res_h, out_sem.at[4])
    result.start()

    @pl.loop(0, pairs)
    def _(p):
        for way in range(2):
            cross_copy(way, p).wait_send()

            @pl.when(has_out(way))
            def _():
                chain_copy(way, p).wait_send()

    @pl.loop(0, heads)
    def _(i):
        for r in range(1, nd):
            part_copy(i, r).wait_send()

    for t in range(groups):

        @pl.loop(1, n)
        def _(r):
            ctx_copy(t, r).wait_send()
            gather_copy(t, r, me).wait_send()

        @pl.loop(0, n)
        def _(r):
            y_copy(t, r, d).wait_send()
            core_copy(t, r, 0, d).wait_send()
            core_copy(t, r, 1, across).wait_send()

    for copy in stores:
        copy.wait()
    result.wait()


def place(nd, groups, hh, rows, a0, a1, a2, a3, maps, b0, b1, b2, b3, qm, km, held, mats, sem, map_sem):
    pairs = ((a0, b0), (a1, b1), (a2, b2), (a3, b3))
    loads = [pltpu.make_async_copy(maps, mats, sem.at[0, 4])]
    loads += [pltpu.make_async_copy(src, held.at[i], sem.at[0, i]) for i, (src, _) in enumerate(pairs)]
    for copy in loads:
        copy.start()
    stores = []
    for i in range(nd):
        for t in range(groups):
            for w, dst in enumerate((qm, km)):
                stores.append(
                    pltpu.make_async_copy(
                        mats.at[i, pl.ds((2 * t + w) * hh, hh)],
                        dst.at[pl.ds(t * hh, hh), pl.ds(i * rows, rows)],
                        map_sem.at[i, t, w],
                    )
                )
    loads[0].wait()
    for copy in stores:
        copy.start()
    for i, (_, dst) in enumerate(pairs):
        loads[1 + i].wait()
        copy = pltpu.make_async_copy(held.at[i], dst, sem.at[1, i])
        copy.start()
        stores.append(copy)
    for copy in stores:
        copy.wait()


def solution(mesh):
    n, nd = mesh.shape["ctx"], mesh.shape["dp"]

    def local(query, key, value, log_decay, grad_out, query_map, key_map):
        heads, width = query_map.shape[0], query_map.shape[1]
        tokens = query.shape[1]
        wide = heads * width
        rows = width // nd
        owned = 2 * heads * rows
        groups = 2 if owned % (2 * 8 * n) == 0 else 1
        hh = heads // groups
        any_spec = pl.BlockSpec(memory_space=pl.ANY)
        vmem_spec = pl.BlockSpec(memory_space=pltpu.VMEM)
        act = pltpu.VMEM((tokens, wide), BF16)
        act32 = pltpu.VMEM((tokens, wide), F32)
        mats = pltpu.VMEM((heads, width, width), F32)
        mats2 = pltpu.VMEM((2, heads, width, width), F32)
        dma = pltpu.SemaphoreType.DMA
        outs = pl.pallas_call(
            functools.partial(kernel, n, nd, groups, heads, width, tokens),
            out_shape=[jax.ShapeDtypeStruct((tokens, wide), BF16)] * 4
            + [jax.ShapeDtypeStruct((nd, owned, width), F32)],
            in_specs=[any_spec, any_spec, any_spec, vmem_spec, any_spec, vmem_spec, vmem_spec],
            out_specs=[any_spec] * 5,
            scratch_shapes=[act] * 8
            + [act32] * 2
            + [act] * 4
            + [
                pltpu.VMEM((heads, tokens), F32),
                pltpu.VMEM((heads, tokens, width), F32),
                pltpu.VMEM((heads, tokens, width), F32),
                pltpu.VMEM((heads, tokens, width), F32),
                pltpu.VMEM((heads, width), F32),
                pltpu.VMEM((heads, width), F32),
            ]
            + [mats] * 4
            + [mats2] * 4
            + [
                pltpu.VMEM((nd, 2 * heads, rows, width), F32),
                pltpu.VMEM((nd - 1, 2 * heads, rows, width), F32),
                pltpu.VMEM((owned, width), F32),
                pltpu.VMEM((groups, n - 1, owned // (groups * n), width), F32),
                pltpu.VMEM((nd, owned, width), F32),
            ]
            + [
                dma((4,)),
                dma((5,)),
                dma((2,)),
                dma((2, heads // 2)),
                dma((2, heads // 2)),
                dma((2, heads // 2)),
                dma((2, heads // 2)),
                dma((nd - 1, heads)),
                dma((nd - 1, heads)),
                dma((groups, n - 1)),
                dma((groups, n - 1)),
                dma((groups, n - 1)),
                dma((groups, n - 1)),
                dma((groups, n)),
                dma((groups, n)),
                dma((groups, 2, n)),
                dma((groups, 2, n)),
            ],
            compiler_params=pltpu.CompilerParams(
                collective_id=0, has_side_effects=True, vmem_limit_bytes=60 * 1024 * 1024
            ),
            cost_estimate=pl.CostEstimate(
                flops=4_000_000_000, bytes_accessed=10_000_000, transcendentals=4_000_000
            ),
        )(query[0], key[0], value[0], log_decay[0], grad_out[0], query_map, key_map)
        maps = outs[4].reshape(nd, 2 * heads, rows, width)
        final = pl.pallas_call(
            functools.partial(place, nd, groups, hh, rows),
            out_shape=[jax.ShapeDtypeStruct((tokens, wide), BF16)] * 4
            + [jax.ShapeDtypeStruct((heads, width, width), F32)] * 2,
            in_specs=[any_spec] * 5,
            out_specs=[any_spec] * 6,
            scratch_shapes=[
                pltpu.VMEM((4, tokens, wide), BF16),
                pltpu.VMEM((nd, 2 * heads, rows, width), F32),
                dma((2, 5)),
                dma((nd, groups, 2)),
            ],
            compiler_params=pltpu.CompilerParams(vmem_limit_bytes=60 * 1024 * 1024),
        )(*outs[:4], maps)
        return tuple(a[None] for a in final[:4]) + tuple(final[4:])

    return jax.shard_map(
        local,
        mesh=mesh,
        in_specs=(
            P("dp", "ctx", None),
            P("dp", "ctx", None),
            P("dp", "ctx", None),
            P("dp", None, "ctx"),
            P("dp", "ctx", None),
            P(),
            P(),
        ),
        out_specs=(
            P("dp", "ctx", None),
            P("dp", "ctx", None),
            P("dp", "ctx", None),
            P("dp", "ctx", None),
            P(),
            P(),
        ),
        check_vma=False,
    )
```

```python
import functools
import math

import jax
import jax.numpy as jnp
from jax import lax
from jax.experimental import pallas as pl
from jax.experimental.pallas import tpu as pltpu
from jax.sharding import PartitionSpec as P

BLOCK = 256
MESH = pl.DeviceIdType.MESH
F32 = jnp.float32
BF16 = jnp.bfloat16


def mm(a, b):
    return lax.dot_general(a, b, (((1,), (0,)), ((), ())), preferred_element_type=F32)


def mm_nt(a, b):
    return lax.dot_general(a, b, (((1,), (1,)), ((), ())), preferred_element_type=F32)


def mm_tn(a, b):
    return lax.dot_general(a, b, (((0,), (0,)), ((), ())), preferred_element_type=F32)


def sigmoid(u):
    return 1.0 / (1.0 + jnp.exp(-u))


def kernel(
    n, nd, groups, heads, width, tokens,
    q_h, k_h, v_h, ld_ref, g_h, qm_ref, km_ref,
    o_h, gq_h, gk_h, gv_h, res_h,
    q_s, k_s, v_s, g_s, o_s, gq_s, gk_s, gv_s,
    sq_s, sk_s, qf_s, kf_s, qd_s, kd_s,
    cum_s, col_s, eq_s, ek_s, mine_s, theirs_s,
    U_s, C_s, u0_s, c1_s, fin_s, fout_s, xout_s, xin_s,
    part_s, pin_s, own_s, cin_s, res_s,
    in_sem, out_sem, dec_sem, ch_send, ch_recv, x_send, x_recv,
    p_send, p_recv, c_send, c_recv, ag_send, ag_recv,
    y_send, y_recv, k_send, k_recv,
):
    scale = 1.0 / (width * math.sqrt(BLOCK))
    me = lax.axis_index("ctx")
    d = lax.axis_index("dp")
    nz = n // 2
    z = me // 2
    x = lax.rem(me, 2)
    partner = me + 1 - 2 * x
    rows = width // nd
    hh = heads // groups

    loads = [
        pltpu.make_async_copy(src, dst, in_sem.at[i])
        for i, (src, dst) in enumerate(((k_h, k_s), (v_h, v_s), (q_h, q_s), (g_h, g_s)))
    ]
    for copy in loads:
        copy.start()

    barrier = pltpu.get_barrier_semaphore()

    @pl.loop(1, n)
    def _(r):
        pl.semaphore_signal(
            barrier, inc=1, device_id=(lax.rem(me + r, n), d), device_id_type=MESH
        )

    for r in range(1, nd):
        pl.semaphore_signal(
            barrier, inc=1, device_id=(me, lax.rem(d + r, nd)), device_id_type=MESH
        )

    cum = ld_ref[...]
    lane = lax.rem(lax.broadcasted_iota(jnp.int32, cum.shape, 1), BLOCK)
    shift = 1
    while shift < BLOCK:
        cum = cum + jnp.where(lane >= shift, pltpu.roll(cum, shift, 1), 0.0)
        shift *= 2
    cum_s[...] = cum
    last = cum[:, BLOCK - 1 : BLOCK] + cum[:, 2 * BLOCK - 1 : 2 * BLOCK]
    mine_s[...] = jnp.broadcast_to(last, mine_s.shape)

    @pl.when(z == 0)
    def _():
        fin_s[0] = jnp.zeros_like(fin_s[0])

    @pl.when(z == nz - 1)
    def _():
        fin_s[1] = jnp.zeros_like(fin_s[1])

    pl.semaphore_wait(barrier, n - 1 + nd - 1)
    decay_copy = pltpu.make_async_remote_copy(
        src_ref=mine_s, dst_ref=theirs_s, send_sem=dec_sem.at[0], recv_sem=dec_sem.at[1],
        device_id=(partner, d), device_id_type=MESH,
    )
    decay_copy.start()
    for copy in loads:
        copy.wait()

    def cols(h):
        return pl.ds(pl.multiple_of(h * width, width), width)

    def blk(b):
        return pl.ds(b * BLOCK, BLOCK)

    def first_pass(h):
        c = cols(h)
        pre = mm(k_s[:, c], km_ref[h])
        sig = sigmoid(pre)
        sk_s[:, c] = sig * (1.0 + pre * (1.0 - sig))
        kf = (pre * sig).astype(BF16)
        kf_s[:, c] = kf
        pre = mm(q_s[:, c], qm_ref[h])
        sig = sigmoid(pre)
        sq_s[:, c] = sig * (1.0 + pre * (1.0 - sig))
        qf = (pre * sig).astype(BF16)
        qf_s[:, c] = qf
        col = jnp.broadcast_to(cum_s[pl.ds(h, 1), :], (width, tokens)).T
        col_s[h] = col
        u, w = [], []
        for b in range(2):
            cb = col[b * BLOCK : (b + 1) * BLOCK]
            tot = cb[BLOCK - 1 : BLOCK]
            part = slice(b * BLOCK, (b + 1) * BLOCK)
            ek = jnp.exp(tot - cb)
            eq = jnp.exp(cb)
            ek_s[h, blk(b), :] = ek
            eq_s[h, blk(b), :] = eq
            kd = (kf[part].astype(F32) * ek).astype(BF16)
            kd_s[blk(b), c] = kd
            u.append(mm_tn(kd, v_s[blk(b), c]))
            qd = (qf[part].astype(F32) * eq).astype(BF16)
            qd_s[blk(b), c] = qd
            w.append(mm_tn(qd, g_s[blk(b), c]))
        d0 = jnp.exp(col[BLOCK - 1 : BLOCK])
        d1 = jnp.exp(col[2 * BLOCK - 1 : 2 * BLOCK])
        U_s[h] = d1 * u[0] + u[1]
        u0_s[h] = u[0]
        C_s[h] = w[0] + d0 * w[1]
        c1_s[h] = w[1]

    def chain_copy(way, p):
        to = z + 1 if way == 0 else z - 1
        to = jnp.clip(to, 0, nz - 1) * 2 + x
        at = pl.ds(2 * p, 2)
        return pltpu.make_async_remote_copy(
            src_ref=fout_s.at[way, at], dst_ref=fin_s.at[way, at],
            send_sem=ch_send.at[way, p], recv_sem=ch_recv.at[way, p],
            device_id=(to, d), device_id_type=MESH,
        )

    def cross_copy(way, p):
        at = pl.ds(2 * p, 2)
        return pltpu.make_async_remote_copy(
            src_ref=xout_s.at[way, at], dst_ref=xin_s.at[way, at],
            send_sem=x_send.at[way, p], recv_sem=x_recv.at[way, p],
            device_id=(partner, d), device_id_type=MESH,
        )

    def is_first(way):
        return (x == 0) if way == 0 else (x == 1)

    def has_in(way):
        return (z > 0) if way == 0 else (z < nz - 1)

    def has_out(way):
        return (z < nz - 1) if way == 0 else (z > 0)

    def chain(way, p):
        @pl.when(has_in(way))
        def _():
            chain_copy(way, p).wait_recv()

        first = is_first(way)
        source = U_s if way == 0 else C_s

        @pl.when(has_out(way))
        def _():
            for h in (2 * p, 2 * p + 1):
                own = mine_s[pl.ds(h, 1), :]
                other = theirs_s[pl.ds(h, 1), :]
                carry = jnp.where(first, jnp.exp(other), 1.0)
                fout_s[way, h] = jnp.exp(own + other) * fin_s[way, h] + carry * source[h]
            chain_copy(way, p).start()

        for h in (2 * p, 2 * p + 1):
            keep = jnp.where(first, jnp.exp(mine_s[pl.ds(h, 1), :]), 1.0)
            xout_s[way, h] = keep * fin_s[way, h] + jnp.where(first, source[h], 0.0)
        cross_copy(way, p).start()

    def entering(way, h):
        other = theirs_s[pl.ds(h, 1), :]
        keep = jnp.where(is_first(way), 1.0, jnp.exp(other))
        return keep * fin_s[way, h] + xin_s[way, h]

    def part_copy(i, r):
        to = lax.rem(d + r, nd)
        at = pl.ds(2 * i, 2)
        return pltpu.make_async_remote_copy(
            src_ref=part_s.at[to, at], dst_ref=pin_s.at[r - 1, at],
            send_sem=p_send.at[r - 1, i], recv_sem=p_recv.at[r - 1, i],
            device_id=(me, to), device_id_type=MESH,
        )

    def keep_part(m, part):
        for i in range(nd):
            part_s[i, m] = part[i * rows : (i + 1) * rows]

    def send_parts(i):
        for r in range(1, nd):
            part_copy(i, r).start()

    half = BLOCK // 2
    iota0 = lax.broadcasted_iota(jnp.int32, (half, half), 0)
    iota1 = lax.broadcasted_iota(jnp.int32, (half, half), 1)
    low, high = slice(0, half), slice(half, BLOCK)

    def stack(a, b, axis):
        return jnp.concatenate([a, b], axis=axis)

    def masked_exp(keep, value):
        return jnp.exp(jnp.where(keep, value, -1e30))

    def finish_q(h):
        c = cols(h)
        state = entering(0, h)
        d0 = jnp.exp(col_s[h, pl.ds(BLOCK - 1, 1), :])
        states = (state.astype(BF16), (d0 * state + u0_s[h]).astype(BF16))
        total = None
        for b in range(2):
            st = states[b]
            cb = col_s[h, blk(b), :]
            row = cum_s[pl.ds(h, 1), blk(b)]
            w0 = masked_exp(iota0 >= iota1, cb[low] - row[:, low])
            w1 = stack(
                jnp.exp(cb[high] - row[:, low]),
                masked_exp(iota0 >= iota1, cb[high] - row[:, high]),
                1,
            )
            qf, kf, v, g = qf_s[blk(b), c], kf_s[blk(b), c], v_s[blk(b), c], g_s[blk(b), c]
            p0 = (mm_nt(qf[low], kf[low]) * w0).astype(BF16)
            p1 = (mm_nt(qf[high], kf) * w1).astype(BF16)
            intra = stack(mm(p0, v[low]), mm(p1, v), 0)
            o_s[blk(b), c] = (scale * (intra + mm(qd_s[blk(b), c], st))).astype(BF16)
            g0 = (mm_nt(g[low], v[low]) * w0).astype(BF16)
            g1 = (mm_nt(g[high], v) * w1).astype(BF16)
            intra = stack(mm(g0, kf[low]), mm(g1, kf), 0)
            gf = scale * (intra + eq_s[h, blk(b), :] * mm_nt(g, st))
            gp = (gf * sq_s[blk(b), c]).astype(BF16)
            gq_s[blk(b), c] = mm_nt(gp, qm_ref[h]).astype(BF16)
            p = mm_tn(q_s[blk(b), c], gp)
            total = p if total is None else total + p
        keep_part((h // hh) * heads + lax.rem(h, hh), total)

    def finish_k(h):
        c = cols(h)
        after = entering(1, h)
        d1 = jnp.exp(col_s[h, pl.ds(2 * BLOCK - 1, 1), :])
        afters = ((c1_s[h] + d1 * after).astype(BF16), after.astype(BF16))
        total = None
        for b in range(2):
            af = afters[b]
            cb = col_s[h, blk(b), :]
            row = cum_s[pl.ds(h, 1), blk(b)]
            w0 = stack(
                masked_exp(iota1 >= iota0, row[:, low] - cb[low]),
                jnp.exp(row[:, high] - cb[low]),
                1,
            )
            w1 = masked_exp(iota1 >= iota0, row[:, high] - cb[high])
            qf, kf, v, g = qf_s[blk(b), c], kf_s[blk(b), c], v_s[blk(b), c], g_s[blk(b), c]
            p0 = (mm_nt(kf[low], qf) * w0).astype(BF16)
            p1 = (mm_nt(kf[high], qf[high]) * w1).astype(BF16)
            intra = stack(mm(p0, g), mm(p1, g[high]), 0)
            gv_s[blk(b), c] = (scale * (intra + mm(kd_s[blk(b), c], af))).astype(BF16)
            g0 = (mm_nt(v[low], g) * w0).astype(BF16)
            g1 = (mm_nt(v[high], g[high]) * w1).astype(BF16)
            intra = stack(mm(g0, qf), mm(g1, qf[high]), 0)
            gf = scale * (intra + ek_s[h, blk(b), :] * mm_nt(v, af))
            gp = (gf * sk_s[blk(b), c]).astype(BF16)
            gk_s[blk(b), c] = mm_nt(gp, km_ref[h]).astype(BF16)
            p = mm_tn(k_s[blk(b), c], gp)
            total = p if total is None else total + p
        keep_part((h // hh) * heads + hh + lax.rem(h, hh), total)

    def first_passes(p):
        first_pass(2 * p)
        first_pass(2 * p + 1)

    def finish(way, p):
        cross_copy(way, p).wait_recv()
        for h in (2 * p, 2 * p + 1):
            (finish_q if way == 0 else finish_k)(h)
        hp = hh // 2
        send_parts((p // hp) * (heads // 2) + way * hp + lax.rem(p, hp))

    size = own_s.shape[0] // (groups * n)

    def piece(t, i):
        return pl.ds(pl.multiple_of((t * n + i) * size, size), size)

    def back(r):
        return lax.rem(me + n - r, n)

    def ctx_copy(t, r):
        to = lax.rem(me + r, n)
        return pltpu.make_async_remote_copy(
            src_ref=own_s.at[piece(t, to)], dst_ref=cin_s.at[t, r - 1],
            send_sem=c_send.at[t, r - 1], recv_sem=c_recv.at[t, r - 1],
            device_id=(to, d), device_id_type=MESH,
        )

    def gather_copy(t, r, i):
        return pltpu.make_async_remote_copy(
            src_ref=res_s.at[d, piece(t, i)], dst_ref=res_s.at[d, piece(t, i)],
            send_sem=ag_send.at[t, r - 1], recv_sem=ag_recv.at[t, r - 1],
            device_id=(lax.rem(me + r, n), d), device_id_type=MESH,
        )

    across = lax.rem(d + 2, nd)
    beside = d + 1 - 2 * lax.rem(d, 2)
    diagonal = lax.rem(beside + 2, nd)

    def y_copy(t, r, whose):
        at = piece(t, back(r))
        return pltpu.make_async_remote_copy(
            src_ref=res_s.at[whose, at], dst_ref=res_s.at[whose, at],
            send_sem=y_send.at[t, r], recv_sem=y_recv.at[t, r],
            device_id=(me, across), device_id_type=MESH,
        )

    def core_copy(t, r, i, whose):
        at = piece(t, back(r))
        return pltpu.make_async_remote_copy(
            src_ref=res_s.at[whose, at], dst_ref=res_s.at[whose, at],
            send_sem=k_send.at[t, i, r], recv_sem=k_recv.at[t, i, r],
            device_id=(me, beside), device_id_type=MESH,
        )

    def reduce_dp(t):
        @pl.loop(0, hh)
        def _(j):
            i = t * hh + j
            at = pl.ds(2 * i, 2)
            total = part_s[d, at]
            for r in range(1, nd):
                part_copy(i, r).wait_recv()
                total = total + pin_s[r - 1, at]
            span = pl.ds(pl.multiple_of(2 * i * rows, 2 * rows), 2 * rows)
            own_s[span, :] = total.reshape(2 * rows, width)

        @pl.loop(1, n)
        def _(r):
            ctx_copy(t, r).start()

    def reduce_ctx(t):
        res_s[d, piece(t, me)] = own_s[piece(t, me)]

        @pl.loop(1, n)
        def _(r):
            ctx_copy(t, r).wait_recv()
            res_s[d, piece(t, me)] = res_s[d, piece(t, me)] + cin_s[t, r - 1]

        @pl.loop(1, n)
        def _(r):
            gather_copy(t, r, me).start()

        y_copy(t, 0, d).start()
        core_copy(t, 0, 0, d).start()

    def gather_ctx(t):
        @pl.loop(1, n)
        def _(r):
            gather_copy(t, r, back(r)).wait_recv()
            y_copy(t, r, d).start()
            core_copy(t, r, 0, d).start()

    def gather_y(t):
        @pl.loop(0, n)
        def _(r):
            y_copy(t, r, across).wait_recv()
            core_copy(t, r, 1, across).start()

    def gather_core(t):
        @pl.loop(0, n)
        def _(r):
            core_copy(t, r, 0, beside).wait_recv()
            core_copy(t, r, 1, diagonal).wait_recv()

    stages = (reduce_dp, reduce_ctx, gather_ctx, gather_y)
    pairs = heads // 2
    steps = pairs + nz + 1
    ready = hh // 2 + nz + 1

    def inside(p):
        return jnp.logical_and(p >= 0, p < pairs)

    @pl.loop(0, steps)
    def _(s):
        pf = s - 1 - z
        pa = s - 1 - (nz - 1 - z)

        @pl.when(s == 1)
        def _():
            decay_copy.wait()

        @pl.when(inside(pf))
        def _():
            chain(0, pf)

        @pl.when(inside(pa))
        def _():
            chain(1, pa)

        @pl.when(s < pairs)
        def _():
            first_passes(s)

        if groups == 2:
            for i, stage in enumerate(stages[:2]):
                pl.when(s == ready + i)(functools.partial(stage, 0))

        @pl.when(inside(pf - 1))
        def _():
            finish(0, pf - 1)

        @pl.when(inside(pa - 1))
        def _():
            finish(1, pa - 1)

        if groups == 2:
            pl.when(s == ready + 1)(functools.partial(gather_ctx, 0))

    stores = [
        pltpu.make_async_copy(src, dst, out_sem.at[i])
        for i, (src, dst) in enumerate(((o_s, o_h), (gq_s, gq_h), (gk_s, gk_h), (gv_s, gv_h)))
    ]
    for copy in stores:
        copy.start()
    if groups == 2:
        reduce_dp(1)
        gather_y(0)
        reduce_ctx(1)
        gather_ctx(1)
        gather_y(1)
    else:
        for stage in stages:
            stage(0)
    for t in range(groups):
        gather_core(t)

    result = pltpu.make_async_copy(res_s, res_h, out_sem.at[4])
    result.start()

    @pl.loop(0, pairs)
    def _(p):
        for way in range(2):
            cross_copy(way, p).wait_send()

            @pl.when(has_out(way))
            def _():
                chain_copy(way, p).wait_send()

    @pl.loop(0, heads)
    def _(i):
        for r in range(1, nd):
            part_copy(i, r).wait_send()

    for t in range(groups):

        @pl.loop(1, n)
        def _(r):
            ctx_copy(t, r).wait_send()
            gather_copy(t, r, me).wait_send()

        @pl.loop(0, n)
        def _(r):
            y_copy(t, r, d).wait_send()
            core_copy(t, r, 0, d).wait_send()
            core_copy(t, r, 1, across).wait_send()

    for copy in stores:
        copy.wait()
    result.wait()


def place(nd, groups, hh, rows, a0, a1, a2, a3, maps, b0, b1, b2, b3, qm, km, held, mats, sem, map_sem):
    pairs = ((a0, b0), (a1, b1), (a2, b2), (a3, b3))
    loads = [pltpu.make_async_copy(maps, mats, sem.at[0, 4])]
    loads += [pltpu.make_async_copy(src, held.at[i], sem.at[0, i]) for i, (src, _) in enumerate(pairs)]
    for copy in loads:
        copy.start()
    stores = []
    for i in range(nd):
        for t in range(groups):
            for w, dst in enumerate((qm, km)):
                stores.append(
                    pltpu.make_async_copy(
                        mats.at[i, pl.ds((2 * t + w) * hh, hh)],
                        dst.at[pl.ds(t * hh, hh), pl.ds(i * rows, rows)],
                        map_sem.at[i, t, w],
                    )
                )
    loads[0].wait()
    for copy in stores:
        copy.start()
    for i, (_, dst) in enumerate(pairs):
        loads[1 + i].wait()
        copy = pltpu.make_async_copy(held.at[i], dst, sem.at[1, i])
        copy.start()
        stores.append(copy)
    for copy in stores:
        copy.wait()


def solution(mesh):
    n, nd = mesh.shape["ctx"], mesh.shape["dp"]

    def local(query, key, value, log_decay, grad_out, query_map, key_map):
        heads, width = query_map.shape[0], query_map.shape[1]
        tokens = query.shape[1]
        wide = heads * width
        rows = width // nd
        owned = 2 * heads * rows
        groups = 2 if owned % (2 * 8 * n) == 0 else 1
        hh = heads // groups
        any_spec = pl.BlockSpec(memory_space=pl.ANY)
        vmem_spec = pl.BlockSpec(memory_space=pltpu.VMEM)
        act = pltpu.VMEM((tokens, wide), BF16)
        act32 = pltpu.VMEM((tokens, wide), F32)
        mats = pltpu.VMEM((heads, width, width), F32)
        mats2 = pltpu.VMEM((2, heads, width, width), F32)
        dma = pltpu.SemaphoreType.DMA
        outs = pl.pallas_call(
            functools.partial(kernel, n, nd, groups, heads, width, tokens),
            out_shape=[jax.ShapeDtypeStruct((tokens, wide), BF16)] * 4
            + [jax.ShapeDtypeStruct((nd, owned, width), F32)],
            in_specs=[any_spec, any_spec, any_spec, vmem_spec, any_spec, vmem_spec, vmem_spec],
            out_specs=[any_spec] * 5,
            scratch_shapes=[act] * 8
            + [act32] * 2
            + [act] * 4
            + [
                pltpu.VMEM((heads, tokens), F32),
                pltpu.VMEM((heads, tokens, width), F32),
                pltpu.VMEM((heads, tokens, width), F32),
                pltpu.VMEM((heads, tokens, width), F32),
                pltpu.VMEM((heads, width), F32),
                pltpu.VMEM((heads, width), F32),
            ]
            + [mats] * 4
            + [mats2] * 4
            + [
                pltpu.VMEM((nd, 2 * heads, rows, width), F32),
                pltpu.VMEM((nd - 1, 2 * heads, rows, width), F32),
                pltpu.VMEM((owned, width), F32),
                pltpu.VMEM((groups, n - 1, owned // (groups * n), width), F32),
                pltpu.VMEM((nd, owned, width), F32),
            ]
            + [
                dma((4,)),
                dma((5,)),
                dma((2,)),
                dma((2, heads // 2)),
                dma((2, heads // 2)),
                dma((2, heads // 2)),
                dma((2, heads // 2)),
                dma((nd - 1, heads)),
                dma((nd - 1, heads)),
                dma((groups, n - 1)),
                dma((groups, n - 1)),
                dma((groups, n - 1)),
                dma((groups, n - 1)),
                dma((groups, n)),
                dma((groups, n)),
                dma((groups, 2, n)),
                dma((groups, 2, n)),
            ],
            compiler_params=pltpu.CompilerParams(
                collective_id=0, has_side_effects=True, vmem_limit_bytes=60 * 1024 * 1024
            ),
            cost_estimate=pl.CostEstimate(
                flops=4_000_000_000, bytes_accessed=10_000_000, transcendentals=4_000_000
            ),
        )(query[0], key[0], value[0], log_decay[0], grad_out[0], query_map, key_map)
        maps = outs[4].reshape(nd, 2 * heads, rows, width)
        final = pl.pallas_call(
            functools.partial(place, nd, groups, hh, rows),
            out_shape=[jax.ShapeDtypeStruct((tokens, wide), BF16)] * 4
            + [jax.ShapeDtypeStruct((heads, width, width), F32)] * 2,
            in_specs=[any_spec] * 5,
            out_specs=[any_spec] * 6,
            scratch_shapes=[
                pltpu.VMEM((4, tokens, wide), BF16),
                pltpu.VMEM((nd, 2 * heads, rows, width), F32),
                dma((2, 5)),
                dma((nd, groups, 2)),
            ],
            compiler_params=pltpu.CompilerParams(vmem_limit_bytes=60 * 1024 * 1024),
        )(*outs[:4], maps)
        return tuple(a[None] for a in final[:4]) + tuple(final[4:])

    return jax.shard_map(
        local,
        mesh=mesh,
        in_specs=(
            P("dp", "ctx", None),
            P("dp", "ctx", None),
            P("dp", "ctx", None),
            P("dp", None, "ctx"),
            P("dp", "ctx", None),
            P(),
            P(),
        ),
        out_specs=(
            P("dp", "ctx", None),
            P("dp", "ctx", None),
            P("dp", "ctx", None),
            P("dp", "ctx", None),
            P(),
            P(),
        ),
        check_vma=False,
    )
```
